512 devices in a mesh: ctx: 16 (over x, z_hi, core), head: 32 (over y, z_lo).
Axes of the slice: x: 4, y: 4, z: 16 (z_hi: 2, z_lo: 8; z = z_hi * 8 + z_lo), core: 2. Of those that a mesh axis runs over, the one named last changes fastest.
Arguments:
- hidden: bfloat16 [2048, 7168], P('ctx', 'head'), may hold values from -6 to 6
- query_down: bfloat16 [7168, 1536], P('head'), may hold values from -0.0625 to 0.0625
- latent_down: bfloat16 [7168, 576], P('head'), may hold values from -0.0625 to 0.0625
- query_gain: float32 [1536], replicated, may hold values from 0.5 to 24, as said below
- latent_gain: float32 [512], replicated, may hold values from 0.25 to 1.75
- query_up: bfloat16 [1536, 24576], P(None, 'head'), may hold values from -0.15625 to 0.15625
- key_absorb: bfloat16 [512, 16384], P(None, 'head'), may hold values from -0.5 to 0.5
- value_absorb: bfloat16 [512, 16384], P(None, 'head'), may hold values from -1 to 1
- out_proj: bfloat16 [16384, 7168], P('head', 'ctx'), may hold values from -0.09375 to 0.09375
- doc_start: int32 [2048], P('ctx'), may hold values from 0 to 2047, as said below
- positions: int32 [2048], P('ctx'), may hold values from 0 to 2047, as said below
Outputs:
- attended: bfloat16 [2048, 7168], P('head', 'ctx')
The draws below stay inside these ranges and needn't reach their ends.
Inputs may be any that keep to these rules, and one draw needn't show every extreme that they name: doc_start never falls along the window, doc_start[i] <= i, doc_start[0] = 0, doc_start[i] = i at the first token of every document, the first document covers at least the first 1152 tokens, and the last token of the window begins a document of its own. positions[i] = i - doc_start[i] in every document but the first; the first document began before the window, and its positions run on from an offset such that its last token has position 2047. `query_gain`: a positive gain for each channel.
All inputs are finite; a program needn't handle non-finite values.
Results may differ from the reference program's by a relative error of at most 0.027.
Values may be sent and summed in bfloat16 or wider, within the bound.
A program may use at most 64 MiB of HBM per device.

```python
import jax
import jax.numpy as jnp
from jax import lax

D = 7168
QRANK = 1536
LATENT = 512
ROPE = 64
NOPE = 128
VDIM = 128
HEADS = 128
TOK_DEV = 128
TOKENS = 2048


def document_cuts(key):
    drawn = jax.random.randint(key, (2,), TOKENS // 2 + TOK_DEV, TOKENS - 1).astype(jnp.int32)
    return jnp.concatenate([drawn, jnp.full((1,), TOKENS - 1, jnp.int32)])


def document_starts(key):
    cuts = document_cuts(key)
    index = jnp.arange(TOKENS, dtype=jnp.int32)
    return jnp.max(jnp.where(cuts[None, :] <= index[:, None], cuts[None, :], 0), axis=1).astype(jnp.int32)


def draw_doc_start(key, part):
    starts = document_starts(key)
    return starts


def draw_positions(key, part):
    starts = document_starts(key)
    first_cut = jnp.min(document_cuts(key))
    offset = (TOKENS - first_cut).astype(jnp.int32)
    index = jnp.arange(TOKENS, dtype=jnp.int32)
    return (index - starts + jnp.where(starts == 0, offset, 0)).astype(jnp.int32)


def draw_query_gain(key, part):
    key = jax.random.fold_in(key, 3)
    values = jax.random.uniform(key, (QRANK,), jnp.float32, 0.5, 1.5)
    return values.astype(jnp.float32)


def draw_hidden(key, part):
    key = jax.random.fold_in(key, 4)
    noise_key, region_key = jax.random.split(key)
    region = jax.random.normal(region_key, (TOKENS // TOK_DEV, D), jnp.float32)
    region = jnp.repeat(region, TOK_DEV, axis=0)
    noise = jax.random.normal(noise_key, (TOKENS, D), jnp.float32)
    values = jnp.clip(0.6 * noise + 0.8 * region, -6.0, 6.0)
    return values.astype(jnp.bfloat16)


def spiked(array, rng, source, target, parts, factor):
    owner, partner = [(jnp.arange(array.shape[axis_at]) // (array.shape[axis_at] // parts)).reshape([-1 if axis == axis_at else 1 for axis in range(array.ndim)]) for axis_at in (source, target)]
    chosen = jax.random.permutation(rng, parts)[partner]
    strong = (owner == chosen) | (owner == (partner + parts // 2) % parts)
    return jnp.where(strong, factor * array, array)


def levels(rng, extent, cuts, smallest, top_value):
    level = 1.0
    for dim, shards_of in cuts:
        heights = jax.random.uniform(jax.random.fold_in(jax.random.fold_in(rng, 6), dim), (shards_of,), jnp.float32, smallest / len(cuts), top_value / len(cuts))
        level = level * jnp.repeat(jnp.exp(heights), extent[dim] // shards_of).reshape((-1,) + (1,) * (len(extent) - 1 - dim))
    return level


def normal_values(rng, shape, deviation, most, pieces=(), kind=jnp.bfloat16):
    array = jax.random.normal(rng, shape, jnp.float32) * deviation
    if len(pieces) > 0:
        array = levels(rng, shape, pieces, -0.22, 0.18) * array
    return jnp.clip(array, min=-most, max=most).astype(kind)


def heavy_noise(stream_key, dims, width, most, cuts, heavy, kind=jnp.bfloat16):
    values = width * jax.random.normal(stream_key, dims, jnp.float32)
    if cuts:
        values = values * levels(stream_key, dims, cuts, -0.22, 0.18)
    return jnp.clip(spiked(values, jax.random.fold_in(stream_key, 3), *heavy), -most, most).astype(kind)


def setup_inputs(seed: int = 0) -> dict:
    key_list = jax.random.split(jax.random.key(seed), 12)
    hidden = draw_hidden(jax.random.fold_in(key_list[11], 71), 0)
    query_down = normal_values(key_list[1], (D, QRANK), D ** -0.5, 0.0625, ((0, 32),))
    latent_down = normal_values(key_list[2], (D, LATENT + ROPE), D ** -0.5, 0.0625, ((0, 32),))
    query_gain = draw_query_gain(jax.random.fold_in(key_list[11], 71), 0)
    latent_gain = jnp.clip(1.0 + 0.15 * jax.random.normal(key_list[4], (LATENT,), jnp.float32), 0.25, 1.75)
    query_up = normal_values(key_list[5], (QRANK, HEADS * (NOPE + ROPE)), QRANK ** -0.5, 0.15625, ((1, 32),))
    key_absorb = normal_values(key_list[6], (LATENT, HEADS * NOPE), NOPE ** -0.5, 0.5, ((1, 32),))
    value_absorb = normal_values(key_list[7], (LATENT, HEADS * VDIM), (LATENT // 16) ** -0.5, 1.0, ((1, 32),))
    out_proj = heavy_noise(key_list[8], (HEADS * VDIM, D), (HEADS * VDIM) ** -0.5, 0.09375, ((0, 32), (1, 16)), (0, 1, 32, 2.75))
    doc_start = draw_doc_start(jax.random.fold_in(key_list[11], 71), 0)
    positions = draw_positions(jax.random.fold_in(key_list[11], 71), 0)
    return {"hidden": hidden, "query_down": query_down, "latent_down": latent_down, "query_gain": query_gain, "latent_gain": latent_gain, "query_up": query_up, "key_absorb": key_absorb, "value_absorb": value_absorb, "out_proj": out_proj, "doc_start": doc_start, "positions": positions}


def rms_norm(values, gain):
    scale = lax.rsqrt(lax.optimization_barrier(jnp.mean(values * values, axis=-1, keepdims=True)) + 1e-06)
    return values * scale * gain

def rotate(values, angles_pos):
    half = values.shape[-1] // 2
    freqs = 10000.0 ** (-2.0 * jnp.arange(half, dtype=jnp.float32) / values.shape[-1])
    angles = angles_pos.astype(jnp.float32)[:, None] * freqs[None, :]
    if values.ndim == 3:
        angles = angles[:, None, :]
    first_half = values[..., :half]
    second_half = values[..., half:]
    cosine = jnp.cos(angles)
    sine = jnp.sin(angles)
    return jnp.concatenate([first_half * cosine - second_half * sine, second_half * cosine + first_half * sine], axis=-1)

def reference(hidden, query_down, latent_down, query_gain, latent_gain, query_up, key_absorb, value_absorb, out_proj, doc_start, positions):
    query_low = jnp.dot(hidden, query_down, preferred_element_type=jnp.float32)
    latent_raw = jnp.dot(hidden, latent_down, preferred_element_type=jnp.float32)
    query_normed = rms_norm(query_low, query_gain).astype(jnp.bfloat16)
    latent = rms_norm(latent_raw[:, :LATENT], latent_gain).astype(jnp.bfloat16)
    key_rot = rotate(latent_raw[:, LATENT:], positions).astype(jnp.bfloat16)
    query_full = jnp.dot(query_normed, query_up, preferred_element_type=jnp.float32).reshape(TOKENS, HEADS, NOPE + ROPE)
    query_nope = query_full[:, :, :NOPE].astype(jnp.bfloat16)
    query_rot = rotate(query_full[:, :, NOPE:], positions).astype(jnp.bfloat16)
    absorb_keys = key_absorb.astype(jnp.float32).reshape(LATENT, HEADS, NOPE)
    query_lat = jnp.einsum('thn,lhn->thl', query_nope.astype(jnp.float32), absorb_keys).astype(jnp.bfloat16)
    keys = jnp.concatenate([latent, key_rot], axis=1)
    queries = jnp.concatenate([query_lat, query_rot], axis=2).transpose(1, 0, 2)
    index = jnp.arange(TOKENS, dtype=jnp.int32)
    visible = (index[None, :] <= index[:, None]) & (index[None, :] >= doc_start[:, None])
    scale = (NOPE + ROPE) ** (-0.5)

    def one_head(head_queries):
        scores = jnp.dot(head_queries, keys.T, preferred_element_type=jnp.float32) * scale
        scores = jnp.where(visible, scores, -1e+30)
        probs = jax.nn.softmax(scores, axis=-1).astype(jnp.bfloat16)
        return jnp.dot(probs, latent, preferred_element_type=jnp.float32).astype(jnp.bfloat16)
    mixed = lax.map(one_head, queries)
    absorb_values = value_absorb.astype(jnp.float32).reshape(LATENT, HEADS, VDIM)
    head_out = jnp.einsum('htl,lhv->thv', mixed.astype(jnp.float32), absorb_values).astype(jnp.bfloat16)
    head_out = head_out.reshape(TOKENS, HEADS * VDIM)
    return jnp.dot(head_out, out_proj, preferred_element_type=jnp.float32).astype(jnp.bfloat16)
```

```python
import jax
import jax.numpy as jnp
from jax import lax
from jax.experimental import pallas as pl
from jax.experimental.pallas import tpu as pltpu
from jax.sharding import PartitionSpec as P

LATENT = 512
ROPE = 64
NOPE = 128
VDIM = 128
QRANK = 1536
NY, NZ = 4, 8
MESH = pl.DeviceIdType.MESH
BF16 = jnp.bfloat16
F32 = jnp.float32


def dot(a, b):
    return jnp.dot(a, b, preferred_element_type=F32)


def place():
    ctx = lax.axis_index("ctx")
    head = lax.axis_index("head")
    return ctx // 4, (ctx // 2) % 2, ctx % 2, head // NZ, head % NZ


def ctx_of(x, zh, core):
    return x * 4 + zh * 2 + core


def send(src, dst, send_sem, recv_sem, ctx, head):
    copy = pltpu.make_async_remote_copy(
        src_ref=src,
        dst_ref=dst,
        send_sem=send_sem,
        recv_sem=recv_sem,
        device_id=(ctx, head),
        device_id_type=MESH,
    )
    copy.start()
    return copy


def greet(partners):
    barrier = pltpu.get_barrier_semaphore()
    for ctx, head in partners:
        pl.semaphore_signal(barrier, inc=1, device_id=(ctx, head), device_id_type=MESH)
    pl.semaphore_wait(barrier, len(partners))


def rows(start, size):
    return pl.ds(pl.multiple_of(start, size), size)


def low_kernel(
    hidden_ref,
    qd_ref,
    ld_ref,
    qg_ref,
    lg_ref,
    cos_ref,
    sin_ref,
    q_ref,
    k_ref,
    y_out,
    y_in,
    own_ref,
    z_out,
    z_in,
    sq_out,
    sq_in,
    kz_ref,
    y_s,
    y_r,
    z_s,
    z_r,
    sq_s,
    sq_r,
    qz_s,
    qz_r,
    qy_s,
    qy_r,
    kz_s,
    kz_r,
    ky_s,
    ky_r,
    kx_s,
    kx_r,
    kc_s,
    kc_r,
):
    x, zh, core, y, z = place()
    ctx, head = ctx_of(x, zh, core), y * NZ + z
    ys = [lax.rem(y + d, NY) for d in range(NY)]
    zs = [lax.rem(z + d, NZ) for d in range(NZ)]
    xs = [lax.rem(x + d, 4) for d in range(4)]
    other = 1 - zh
    far = ctx_of(x, other, core)
    partners = [(ctx, ys[d] * NZ + z) for d in range(1, NY)]
    partners += [(ctx, y * NZ + zs[d]) for d in range(1, NZ)]
    partners += [(far, y * NZ + zs[d]) for d in range(NZ)]
    partners += [(ctx_of(xs[d], zh, core), head) for d in range(1, 4)]
    partners += [(ctx_of(x, zh, 1 - core), head)]
    greet(partners)

    hid = hidden_ref[...]
    rot = dot(hid, ld_ref[:, LATENT:])
    rot = jnp.concatenate([rot, jnp.zeros_like(rot)], axis=1)
    waits = []
    for d in (2, 1, 3, 0):
        part = [
            dot(hid, qd_ref[:, rows(ys[d] * 384, 384)]),
            dot(hid, ld_ref[:, rows(ys[d] * 128, 128)]),
            rot,
        ]
        if d:
            for at, piece in zip((0, 384, 512), part):
                y_out[d - 1, :, at : at + piece.shape[1]] = piece.astype(BF16)
            waits.append(
                send(y_out.at[d - 1], y_in.at[d - 1], y_s.at[d - 1], y_r.at[d - 1], ctx, ys[d] * NZ + z)
            )
        else:
            for at, piece in zip((0, 384, 512), part):
                own_ref[:, at : at + piece.shape[1]] = piece
    for copy in waits:
        copy.wait()
    total = own_ref[...]
    for d in range(3):
        total = total + y_in[d].astype(F32)
    own_ref[...] = total
    for i in range(NZ):
        z_out[i] = total[16 * i : 16 * i + 16].astype(BF16)
    waits = []
    for d in (4, 5, 3, 6, 2, 7, 1):
        waits.append(
            send(z_out.at[zs[d]], z_in.at[d - 1], z_s.at[d - 1], z_r.at[d - 1], ctx, y * NZ + zs[d])
        )
    for copy in waits:
        copy.wait()
    mine = own_ref[rows(z * 16, 16), :]
    for d in range(NZ - 1):
        mine = mine + z_in[d].astype(F32)
    q_low, lat, rot = mine[:, :384], mine[:, 384:512], mine[:, 512:]

    lane = lax.broadcasted_iota(jnp.int32, (16, 128), 1)
    q_sq = jnp.sum(q_low * q_low, axis=1, keepdims=True)
    l_sq = jnp.sum(lat * lat, axis=1, keepdims=True)
    sq_out[...] = jnp.where(lane < 64, q_sq, l_sq)
    waits = []
    for d in range(1, NY):
        waits.append(
            send(sq_out, sq_in.at[d - 1], sq_s.at[d - 1], sq_r.at[d - 1], ctx, ys[d] * NZ + z)
        )
    half = ROPE // 2
    here = rows(z * 16, 16)
    swapped = jnp.concatenate([rot[:, half:ROPE], rot[:, :half]], axis=1)
    turned = rot[:, :ROPE] * cos_ref[here, :] + swapped * sin_ref[here, :]
    turned = jnp.concatenate([turned, jnp.zeros_like(turned)], axis=1)
    for copy in waits:
        copy.wait()
    total = sq_out[...] + sq_in[0] + sq_in[1] + sq_in[2]
    q_scale = lax.rsqrt(total[:, 0:1] / QRANK + 1e-06)
    l_scale = lax.rsqrt(total[:, 64:65] / LATENT + 1e-06)
    q_cols = rows(y * 384, 384)
    l_cols = rows(y * 128, 128)
    kz_ref[zh, here, 0:128] = (lat * l_scale * lg_ref[:, l_cols]).astype(BF16)
    kz_ref[zh, here, 128:256] = turned.astype(BF16)
    q_ref[here, q_cols] = (q_low * q_scale * qg_ref[:, q_cols]).astype(BF16)

    kz, qz = [], []
    mine = kz_ref.at[zh, here]
    for d in (4, 5, 3, 6, 2, 7, 1):
        kz.append(send(mine, mine, kz_s.at[d], kz_r.at[d], ctx, y * NZ + zs[d]))
    for d in range(NZ):
        kz.append(send(mine, mine, kz_s.at[NZ + d], kz_r.at[NZ + d], far, y * NZ + zs[d]))
    mine = q_ref.at[here, q_cols]
    for d in (4, 5, 3, 6, 2, 7, 1):
        qz.append(send(mine, mine, qz_s.at[d], qz_r.at[d], ctx, y * NZ + zs[d]))
    for copy in kz:
        copy.wait()
    blocks = [rows(ctx_of(x, i, core) * 128, 128) for i in range(2)]
    ky, kc = [], []
    for i in range(2):
        k_ref[blocks[i], l_cols] = kz_ref[i, :, 0:128]
        k_ref[blocks[i], LATENT:640] = kz_ref[i, :, 128:256]
        mine = k_ref.at[blocks[i], l_cols]
        for d in (2, 1, 3):
            ky.append(send(mine, mine, ky_s.at[i, d], ky_r.at[i, d], ctx, ys[d] * NZ + z))
    for copy in ky:
        copy.wait()
    kx = [[], [], [], []]
    across = ctx_of(x, zh, 1 - core)
    for i in range(2):
        mine = k_ref.at[blocks[i], :]
        for d in (2, 1, 3):
            kx[d].append(
                send(mine, mine, kx_s.at[i, d], kx_r.at[i, d], ctx_of(xs[d], zh, core), head)
            )
        kc.append(send(mine, mine, kc_s.at[i, 0], kc_r.at[i, 0], across, head))
    for copy in qz:
        copy.wait()
    qy = []
    mine = q_ref.at[:, q_cols]
    for d in (2, 1, 3):
        qy.append(send(mine, mine, qy_s.at[d], qy_r.at[d], ctx, ys[d] * NZ + z))
    for d in (1, 3, 2):
        for i in range(2):
            kx[d][i].wait()
            block = rows(ctx_of(lax.rem(x + 4 - d, 4), i, core) * 128, 128)
            mine = k_ref.at[block, :]
            kc.append(send(mine, mine, kc_s.at[i, d], kc_r.at[i, d], across, head))
    for copy in qy + kc:
        copy.wait()


def low_call(hidden, query_down, latent_down, query_gain, latent_gain, cosine, sine):
    dma = pltpu.SemaphoreType.DMA
    vmem = pl.BlockSpec(memory_space=pltpu.VMEM)
    scratch = [
        pltpu.VMEM((3, 128, 640), BF16),
        pltpu.VMEM((3, 128, 640), BF16),
        pltpu.VMEM((128, 640), F32),
        pltpu.VMEM((8, 16, 640), BF16),
        pltpu.VMEM((7, 16, 640), BF16),
        pltpu.VMEM((16, 128), F32),
        pltpu.VMEM((3, 16, 128), F32),
        pltpu.VMEM((2, 128, 256), BF16),
    ]
    for shape in [(3,), (7,), (3,), (8,), (4,), (16,), (2, 4), (2, 4), (2, 4)]:
        scratch += [dma(shape), dma(shape)]
    return pl.pallas_call(
        low_kernel,
        out_shape=(
            jax.ShapeDtypeStruct((128, QRANK), BF16),
            jax.ShapeDtypeStruct((2048, 640), BF16),
        ),
        in_specs=[vmem] * 7,
        out_specs=(vmem, vmem),
        scratch_shapes=scratch,
        compiler_params=pltpu.CompilerParams(
            collective_id=0, has_side_effects=True, vmem_limit_bytes=32 * 1024 * 1024
        ),
        name="low_rank",
    )(hidden, query_down, latent_down, query_gain, latent_gain, cosine, sine)


def out_kernel(
    ho_ref,
    w_ref,
    out_ref,
    g_ref,
    y_out,
    y_in,
    own_ref,
    z_out,
    z_in,
    h_s,
    h_r,
    x_s,
    x_r,
    c_s,
    c_r,
    y_s,
    y_r,
    z_s,
    z_r,
):
    x, zh, core, y, z = place()
    ctx, head = ctx_of(x, zh, core), y * NZ + z
    ys = [lax.rem(y + d, NY) for d in range(NY)]
    zs = [lax.rem(z + d, NZ) for d in range(NZ)]
    xs = [lax.rem(x + d, 4) for d in range(4)]
    other = 1 - zh
    far = ctx_of(x, other, core)
    across = ctx_of(x, zh, 1 - core)
    partners = [(ctx, ys[d] * NZ + z) for d in range(1, NY)]
    partners += [(ctx, y * NZ + zs[d]) for d in range(1, NZ)]
    partners += [(ctx_of(xs[d], zh, core), head) for d in range(1, 4)]
    partners += [(far, head), (across, head)]
    greet(partners)

    def block(d, half):
        return g_ref.at[rows(ctx_of(lax.rem(x + 4 - d, 4), half, core) * 128, 128), :]

    g_ref[rows(ctx * 128, 128), :] = ho_ref[...]
    mine = block(0, zh)
    over = send(mine, mine, h_s, h_r, far, head)
    kx, kc = {}, []
    for half, first in ((zh, 0), (other, 1)):
        if first:
            over.wait()
        mine = block(0, half)
        for d in (2, 1, 3):
            kx[first, d] = send(
                mine, mine, x_s.at[first, d], x_r.at[first, d], ctx_of(xs[d], zh, core), head
            )
        kc.append(send(mine, mine, c_s.at[first, 0], c_r.at[first, 0], across, head))
    for half, first in ((zh, 0), (other, 1)):
        for d in (1, 3, 2):
            kx[first, d].wait()
            mine = block(d, half)
            kc.append(send(mine, mine, c_s.at[first, d], c_r.at[first, d], across, head))
    for copy in kc:
        copy.wait()

    w = w_ref[...]
    waits = []
    for d in (2, 1, 3, 0):

        @pl.loop(0, 4)
        def _(i):
            at = rows(i * 128, 128)
            part = dot(g_ref[rows(ys[d] * 512 + i * 128, 128), :], w)
            if d:
                y_out[d - 1, at, :] = part.astype(BF16)
            else:
                own_ref[at, :] = part

        if d:
            waits.append(
                send(y_out.at[d - 1], y_in.at[d - 1], y_s.at[d - 1], y_r.at[d - 1], ctx, ys[d] * NZ + z)
            )
    for copy in waits:
        copy.wait()

    @pl.loop(0, NZ)
    def _(i):
        at = rows(i * 64, 64)
        total = own_ref[at, :]
        for d in range(3):
            total = total + y_in[d, at, :].astype(F32)
        own_ref[at, :] = total
        z_out[i] = total.astype(BF16)

    waits = []
    for d in (4, 5, 3, 6, 2, 7, 1):
        waits.append(
            send(z_out.at[zs[d]], z_in.at[d - 1], z_s.at[d - 1], z_r.at[d - 1], ctx, y * NZ + zs[d])
        )
    for copy in waits:
        copy.wait()
    total = own_ref[rows(z * 64, 64), :]
    for d in range(NZ - 1):
        total = total + z_in[d].astype(F32)
    out_ref[...] = total.astype(BF16)


def out_call(head_out, out_proj):
    dma = pltpu.SemaphoreType.DMA
    vmem = pl.BlockSpec(memory_space=pltpu.VMEM)
    cols = out_proj.shape[1]
    scratch = [
        pltpu.VMEM((2048, 512), BF16),
        pltpu.VMEM((3, 512, cols), BF16),
        pltpu.VMEM((3, 512, cols), BF16),
        pltpu.VMEM((512, cols), F32),
        pltpu.VMEM((8, 64, cols), BF16),
        pltpu.VMEM((7, 64, cols), BF16),
        dma,
        dma,
    ]
    for shape in [(2, 4), (2, 4), (3,), (7,)]:
        scratch += [dma(shape), dma(shape)]
    return pl.pallas_call(
        out_kernel,
        out_shape=jax.ShapeDtypeStruct((64, cols), BF16),
        in_specs=[vmem] * 2,
        out_specs=vmem,
        scratch_shapes=scratch,
        compiler_params=pltpu.CompilerParams(
            collective_id=1, has_side_effects=True, vmem_limit_bytes=32 * 1024 * 1024
        ),
        name="out_sum",
    )(head_out, out_proj)


def body(
    hidden,
    query_down,
    latent_down,
    query_gain,
    latent_gain,
    query_up,
    key_absorb,
    value_absorb,
    out_proj,
    doc_start,
    positions,
):
    tok_rows = hidden.shape[0]
    heads_here = query_up.shape[1] // (NOPE + ROPE)
    half = ROPE // 2
    freqs = 10000.0 ** (-2.0 * jnp.arange(half, dtype=F32) / ROPE)
    angles = positions.astype(F32)[:, None] * freqs[None, :]
    cosine, sine = jnp.cos(angles), jnp.sin(angles)
    cosine = jnp.concatenate([cosine, cosine], axis=1)
    sine = jnp.concatenate([-sine, sine], axis=1)
    query_normed, keys = low_call(
        hidden, query_down, latent_down, query_gain[None, :], latent_gain[None, :], cosine, sine
    )
    keys = keys[:, : LATENT + ROPE]
    query_full = dot(query_normed, query_up).reshape(tok_rows, heads_here, NOPE + ROPE)
    query_nope = query_full[:, :, :NOPE].astype(BF16)
    raw = query_full[:, :, NOPE:]
    swapped = jnp.concatenate([raw[..., half:], raw[..., :half]], axis=-1)
    query_rot = (raw * cosine[:, None, :] + swapped * sine[:, None, :]).astype(BF16)
    query_lat = jnp.einsum(
        "thn,lhn->thl",
        query_nope,
        key_absorb.reshape(LATENT, heads_here, NOPE),
        preferred_element_type=F32,
    ).astype(BF16)
    queries = jnp.concatenate([query_lat, query_rot], axis=2).reshape(
        tok_rows * heads_here, LATENT + ROPE
    )
    first_row = lax.axis_index("ctx") * tok_rows
    query_index = jnp.repeat(first_row + jnp.arange(tok_rows, dtype=jnp.int32), heads_here)
    query_doc = jnp.repeat(doc_start, heads_here)
    scale = (NOPE + ROPE) ** (-0.5)
    key_index = jnp.arange(keys.shape[0], dtype=jnp.int32)
    scores = (
        lax.dot_general(queries, keys, (((1,), (1,)), ((), ())), preferred_element_type=F32) * scale
    )
    visible = (key_index[None, :] <= query_index[:, None]) & (
        key_index[None, :] >= query_doc[:, None]
    )
    scores = jnp.where(visible, scores, -1e30)
    top = jnp.max(scores, axis=1)
    expo = jnp.where(visible, jnp.exp(scores - top[:, None]), 0.0)
    total = jnp.sum(expo, axis=1)
    weighted = dot(expo.astype(BF16), keys[:, :LATENT])
    mixed = (weighted / total[:, None]).astype(BF16).reshape(tok_rows, heads_here, LATENT)
    head_out = jnp.einsum(
        "thl,lhv->thv",
        mixed,
        value_absorb.reshape(LATENT, heads_here, VDIM),
        preferred_element_type=F32,
    ).astype(BF16)
    return out_call(head_out.reshape(tok_rows, heads_here * VDIM), out_proj)


def solution(mesh):
    in_specs = (
        P("ctx", "head"),
        P("head", None),
        P("head", None),
        P(),
        P(),
        P(None, "head"),
        P(None, "head"),
        P(None, "head"),
        P("head", "ctx"),
        P("ctx"),
        P("ctx"),
    )
    out_specs = P("head", "ctx")
    return jax.shard_map(body, mesh=mesh, in_specs=in_specs, out_specs=out_specs, check_vma=False)
```

```python
import jax
import jax.numpy as jnp
import numpy as np
from jax import lax
from jax.experimental import pallas as pl
from jax.experimental.pallas import tpu as pltpu
from jax.sharding import PartitionSpec as P

LATENT = 512
ROPE = 64
NOPE = 128
VDIM = 128
QRANK = 1536
NX, NY, NZ = 4, 4, 8
KEY = LATENT + 2 * ROPE
SCALE = (NOPE + ROPE) ** (-0.5)
MESH = pl.DeviceIdType.MESH
BF16 = jnp.bfloat16
F32 = jnp.float32
FAR_FIRST = (4, 5, 3, 6, 2, 7, 1)
N_WIRES = 176


def dot(a, b):
    return jnp.dot(a, b, preferred_element_type=F32)


def dot_t(a, b):
    return lax.dot_general(a, b, (((1,), (1,)), ((), ())), preferred_element_type=F32)


def rows(start, size):
    return pl.ds(pl.multiple_of(start, size), size)


def ctx_of(x, zh, core):
    return x * 4 + zh * 2 + core


class Wires:
    def __init__(self, send_sems, recv_sems):
        self.send_sems, self.recv_sems, self.used = send_sems, recv_sems, 0

    def send(self, src, dst, to):
        at = self.used
        self.used += 1
        copy = pltpu.make_async_remote_copy(
            src_ref=src,
            dst_ref=dst,
            send_sem=self.send_sems.at[at],
            recv_sem=self.recv_sems.at[at],
            device_id=to,
            device_id_type=MESH,
        )
        copy.start()
        return copy


def wait_all(copies):
    for copy in copies:
        copy.wait()


def kernel(
    hidden_hbm,
    qd_hbm,
    ld_hbm,
    qg_hbm,
    lg_hbm,
    qup_hbm,
    ka_hbm,
    va_hbm,
    wo_hbm,
    doc_hbm,
    pos_hbm,
    freq_hbm,
    out_ref,
    hidden_ref,
    qd_ref,
    ld_ref,
    qg_ref,
    lg_ref,
    qup_ref,
    ka_ref,
    va_ref,
    wo_ref,
    doc_ref,
    pos_ref,
    freq_ref,
    gain_ref,
    lgain_ref,
    cos_ref,
    sin_ref,
    kv_out,
    kv_in,
    q_out,
    q_in,
    kv_own,
    q_own,
    kvz_out,
    kvz_in,
    qz_out,
    qz_in,
    sq_out,
    sq_in,
    kz_ref,
    q_ref,
    k_ref,
    qc_ref,
    s_ref,
    ho_ref,
    g_ref,
    own_ref,
    z_out,
    z_in,
    fin_out,
    fin_ref,
    load_sems,
    send_sems,
    recv_sems,
):
    ctx = lax.axis_index("ctx")
    head = lax.axis_index("head")
    x, zh, core = ctx // 4, (ctx // 2) % 2, ctx % 2
    y, z = head // NZ, head % NZ
    ys = [lax.rem(y + d, NY) for d in range(NY)]
    zs = [lax.rem(z + d, NZ) for d in range(NZ)]
    other = 1 - zh
    far = ctx_of(x, other, core)
    to_y = [(ctx, ys[d] * NZ + z) for d in range(NY)]
    to_z = [(ctx, y * NZ + zs[d]) for d in range(NZ)]
    to_far = [(far, y * NZ + zs[d]) for d in range(NZ)]
    to_x = [(ctx_of(lax.rem(x + d, NX), zh, core), head) for d in range(NX)]
    to_core = (ctx_of(x, zh, 1 - core), head)
    wires = Wires(send_sems, recv_sems)

    loads = {}
    for i, (name, src, dst) in enumerate(
        [
            ("hidden", hidden_hbm, hidden_ref),
            ("ld", ld_hbm, ld_ref),
            ("qd", qd_hbm, qd_ref),
            ("qg", qg_hbm, qg_ref),
            ("lg", lg_hbm, lg_ref),
            ("pos", pos_hbm, pos_ref),
            ("doc", doc_hbm, doc_ref),
            ("freq", freq_hbm, freq_ref),
            ("qup", qup_hbm, qup_ref),
            ("ka", ka_hbm, ka_ref),
            ("va", va_hbm, va_ref),
            ("wo", wo_hbm, wo_ref.at[y]),
        ]
    ):
        loads[name] = pltpu.make_async_copy(src, dst, load_sems.at[i])
        loads[name].start()
    barrier = pltpu.get_barrier_semaphore()
    partners = to_y[1:] + to_z[1:] + to_far + to_x[1:] + [to_core]
    for to in partners:
        pl.semaphore_signal(barrier, inc=1, device_id=to, device_id_type=MESH)
    pl.semaphore_wait(barrier, len(partners))

    loads["hidden"].wait()
    loads["ld"].wait()
    hid = hidden_ref[...]
    rot = dot(hid, ld_ref[:, LATENT:])
    rot = jnp.concatenate([rot, jnp.zeros_like(rot)], axis=1)
    kv_y = []
    for d in (2, 1, 3):
        kv_out[d - 1, :, 0:128] = dot(hid, ld_ref[:, rows(ys[d] * 128, 128)]).astype(BF16)
        kv_out[d - 1, :, 128:256] = rot.astype(BF16)
        kv_y.append(wires.send(kv_out.at[d - 1], kv_in.at[d - 1], to_y[d]))
    l_cols = rows(y * 128, 128)
    q_cols = rows(y * 384, 384)
    kv_own[:, 0:128] = dot(hid, ld_ref[:, l_cols])
    kv_own[:, 128:256] = rot
    loads["qd"].wait()
    q_y = []
    for d in (2, 1, 3):
        q_out[d - 1] = dot(hid, qd_ref[:, rows(ys[d] * 384, 384)]).astype(BF16)
        q_y.append(wires.send(q_out.at[d - 1], q_in.at[d - 1], to_y[d]))
    q_own[...] = dot(hid, qd_ref[:, q_cols])

    loads["pos"].wait()
    loads["freq"].wait()
    angles = freq_ref[...] * pos_ref[...].astype(F32)[None, :]
    cosine, sine = jnp.cos(angles), jnp.sin(angles)
    cos_ref[...] = jnp.concatenate([cosine, cosine, cosine, cosine], axis=0).T
    sin_ref[...] = jnp.concatenate([-sine, sine, -sine, sine], axis=0).T
    loads["qg"].wait()
    loads["lg"].wait()
    gain_ref[...] = qg_ref[...][None, :]
    lgain_ref[...] = lg_ref[...][None, :]

    def over_y(copies, own, received):
        wait_all(copies)
        total = own[...]
        for d in range(NY - 1):
            total = total + received[d].astype(F32)
        own[...] = total
        return total

    def to_all_z(total, out, received):
        for i in range(NZ):
            out[i] = total[16 * i : 16 * i + 16].astype(BF16)
        return [wires.send(out.at[zs[d]], received.at[d - 1], to_z[d]) for d in FAR_FIRST]

    here = rows(z * 16, 16)

    def over_z(copies, own, received):
        wait_all(copies)
        total = own[here, :]
        for d in range(NZ - 1):
            total = total + received[d].astype(F32)
        return total

    def square(i, values):
        total = jnp.sum(values * values, axis=1, keepdims=True)
        sq_out[i] = jnp.broadcast_to(total, (16, 128))
        return [wires.send(sq_out.at[i], sq_in.at[i, d - 1], to_y[d]) for d in (2, 1, 3)]

    def scale_of(i, copies, count):
        wait_all(copies)
        total = sq_out[i] + sq_in[i, 0] + sq_in[i, 1] + sq_in[i, 2]
        return lax.rsqrt(total[:, 0:1] / count + 1e-06)

    kv_z = to_all_z(over_y(kv_y, kv_own, kv_in), kvz_out, kvz_in)
    q_z = to_all_z(over_y(q_y, q_own, q_in), qz_out, qz_in)
    mine = over_z(kv_z, kv_own, kvz_in)
    lat, rot = mine[:, :128], mine[:, 128:]
    kv_sq = square(0, lat)
    half = ROPE // 2
    swapped = jnp.concatenate([rot[:, half:ROPE], rot[:, :half]], axis=1)
    turned = rot[:, :ROPE] * cos_ref[here, :ROPE] + swapped * sin_ref[here, :ROPE]
    kz_ref[zh, here, 128:256] = jnp.concatenate([turned, jnp.zeros_like(turned)], axis=1).astype(BF16)
    q_low = over_z(q_z, q_own, qz_in)
    q_sq = square(1, q_low)

    l_scale = scale_of(0, kv_sq, LATENT)
    kz_ref[zh, here, 0:128] = (lat * l_scale * lgain_ref[:, l_cols]).astype(BF16)
    piece = kz_ref.at[zh, here]
    kz = [wires.send(piece, piece, to_z[d]) for d in FAR_FIRST]
    kz += [wires.send(piece, piece, to_far[d]) for d in range(NZ)]
    q_scale = scale_of(1, q_sq, QRANK)
    q_ref[here, q_cols] = (q_low * q_scale * gain_ref[:, q_cols]).astype(BF16)
    piece = q_ref.at[here, q_cols]
    qz = [wires.send(piece, piece, to_z[d]) for d in FAR_FIRST]

    def key_rows(d, i):
        return rows(ctx_of(lax.rem(x + NX - d, NX), i, core) * 128, 128)

    wait_all(kz)
    for i in range(2):
        k_ref[key_rows(0, i), l_cols] = kz_ref[i, :, 0:128]
        k_ref[key_rows(0, i), LATENT:KEY] = kz_ref[i, :, 128:256]

    def key_over_y(d, i):
        piece = k_ref.at[key_rows(d, i), l_cols]
        return [wires.send(piece, piece, to_y[e]) for e in (2, 1, 3)]

    first_y = key_over_y(0, 0)
    second_x, second_y = {}, {}
    for d in (2, 1, 3):
        second_x[d] = []
        for cols in (l_cols, pl.ds(LATENT, 128)):
            piece = k_ref.at[key_rows(0, 1), cols]
            second_x[d].append(wires.send(piece, piece, to_x[d]))
    second_y[0] = key_over_y(0, 1)
    wait_all(qz)
    piece = q_ref.at[:, q_cols]
    q_all = [wires.send(piece, piece, to_y[d]) for d in (2, 1, 3)]
    wait_all(first_y)
    first_x = {}
    for d in (2, 1, 3):
        piece = k_ref.at[key_rows(0, 0), :]
        first_x[d] = [wires.send(piece, piece, to_x[d])]
    for d in (1, 3, 2):
        wait_all(second_x[d])
        second_y[d] = key_over_y(d, 1)
    loads["wo"].wait()
    weights = [wires.send(wo_ref.at[y], wo_ref.at[y], to_y[d]) for d in (2, 1, 3)]

    key_core = {}

    def key_to_core(d):
        if d:
            wait_all(first_x[d])
        wait_all(second_y[d])
        key_core[d] = []
        for i in range(2):
            piece = k_ref.at[key_rows(d, i), :]
            key_core[d].append(wires.send(piece, piece, to_core))

    for name in ("qup", "ka", "va", "doc"):
        loads[name].wait()
    wait_all(q_all)
    key_to_core(0)
    full = dot(q_ref[...], qup_ref[...])
    cosine, sine = cos_ref[:, :ROPE], sin_ref[:, :ROPE]
    for h in range(4):
        at = h * (NOPE + ROPE)
        nope = full[:, at : at + NOPE].astype(BF16)
        raw = full[:, at + NOPE : at + NOPE + ROPE]
        swapped = jnp.concatenate([raw[:, half:], raw[:, :half]], axis=1)
        turned = raw * cosine + swapped * sine
        low = dot_t(nope, ka_ref[:, h * NOPE : (h + 1) * NOPE])
        mine = slice(h * 128, h * 128 + 128)
        qc_ref[mine, :LATENT] = low.astype(BF16)
        qc_ref[mine, LATENT:] = jnp.concatenate([turned, jnp.zeros_like(turned)], axis=1).astype(BF16)

    doc = jnp.broadcast_to(doc_ref[...].astype(F32)[None, :], (128, 128)).T[:, 0:1].astype(jnp.int32)
    query_index = ctx * 128 + lax.broadcasted_iota(jnp.int32, (128, 512), 0)
    key_lane = lax.broadcasted_iota(jnp.int32, (128, 512), 1)
    top = [None] * 4

    def scores(d):
        wait_all(key_core[d])
        at = rows(lax.rem(x + NX - d, NX) * 512, 512)
        key_index = key_lane + lax.rem(x + NX - d, NX) * 512
        bias = jnp.where((key_index <= query_index) & (key_index >= doc), 0.0, -1e30)
        block = dot_t(qc_ref[...], k_ref[at, :])
        for h in range(4):
            mine = slice(h * 128, h * 128 + 128)
            values = block[mine] * SCALE + bias
            s_ref[mine, at] = values
            most = jnp.max(values, axis=1, keepdims=True)
            top[h] = most if top[h] is None else jnp.maximum(top[h], most)

    key_to_core(1)
    scores(0)
    key_to_core(3)
    scores(1)
    key_to_core(2)
    scores(3)
    scores(2)

    here_zc, far_zc = zh * 2 + core, other * 2 + core
    cols = rows(y * 256, 256)

    def mix(pair):
        mine = slice(pair * 256, pair * 256 + 256)
        most = jnp.concatenate([top[2 * pair], top[2 * pair + 1]], axis=0)
        weighted = jnp.zeros((256, LATENT), F32)
        total = jnp.zeros((256, 1), F32)
        for j in range(4):
            expo = jnp.exp(s_ref[mine, 512 * j : 512 * j + 512] - most)
            total = total + jnp.sum(expo, axis=1, keepdims=True)
            weighted = weighted + dot(expo.astype(BF16), k_ref[512 * j : 512 * j + 512, :LATENT])
        mixed = (weighted / total).astype(BF16)
        for i in range(2):
            at = (2 * pair + i) * VDIM
            result = dot(mixed[128 * i : 128 * i + 128], va_ref[:, at : at + VDIM]).astype(BF16)
            for part in range(4):
                for side in range(2):
                    first = 64 * side + 16 * part
                    ho_ref[pair, part, side, :, 128 * i : 128 * i + 128] = result[first : first + 16]
        g_ref[pair, here_zc, :, x, :, cols] = ho_ref[pair, y]
        spot = g_ref.at[pair, here_zc, :, x, :, cols]
        return [wires.send(ho_ref.at[pair, ys[d]], spot, to_y[d]) for d in (2, 1, 3)]

    def block(pair, zc, d):
        return g_ref.at[pair, zc, :, lax.rem(x + NX - d, NX)]

    def spread(pair, zc, over_x):
        piece = block(pair, zc, 0)
        for d in (2, 1, 3):
            over_x[pair, zc is far_zc, d] = wires.send(piece, piece, to_x[d])
        return wires.send(piece, piece, to_core)

    over_x, over_core, over_far = {}, [], {}

    def launch(pair, copies):
        wait_all(copies)
        piece = block(pair, here_zc, 0)
        over_far[pair] = wires.send(piece, piece, to_far[0])
        over_core.append(spread(pair, here_zc, over_x))

    handed = mix(0)
    second = mix(1)
    launch(0, handed)
    launch(1, second)
    for pair in range(2):
        over_far[pair].wait()
        over_core.append(spread(pair, far_zc, over_x))
    for pair in range(2):
        for zc in (here_zc, far_zc):
            for d in (1, 3, 2):
                over_x[pair, zc is far_zc, d].wait()
                piece = block(pair, zc, d)
                over_core.append(wires.send(piece, piece, to_core))
    wait_all(over_core)
    wait_all(weights)

    pair_at, odd = z // 2, z % 2
    sums = {}
    for k in (2, 1, 3, 0):
        zc = lax.rem(pair_at + k, 4)
        total = jnp.zeros((128, out_ref.shape[1]), F32)
        for pair in range(2):
            tokens = g_ref[pair, zc].reshape(128, 1024)
            for i in range(NY):
                total = total + dot(
                    tokens[:, 256 * i : 256 * i + 256], wo_ref[i, 256 * pair : 256 * pair + 256, :]
                )
        for side in range(2):
            part = total[64 * side : 64 * side + 64]
            part = jnp.concatenate([part[:32], part[32:]], axis=1)
            z_out[k, side] = part.astype(BF16)
            if k == 0:
                own_ref[side] = part
        for flip in (0, 1):
            if k or flip:
                side = odd + flip - 2 * odd * flip
                to = (ctx, y * NZ + zc * 2 + side)
                sums[k, flip] = wires.send(z_out.at[k, side], z_in.at[k, flip], to)
    total = own_ref[odd]
    for key in ((0, 1), (1, 0), (1, 1), (3, 0), (3, 1), (2, 0), (2, 1)):
        sums[key].wait()
        total = total + z_in[key].astype(F32)
    width = out_ref.shape[1]
    result = jnp.concatenate([total[:, :width], total[:, width:]], axis=0).astype(BF16)
    for i in range(NX):
        fin_out[i] = result[16 * i : 16 * i + 16]
    fin_ref[y] = fin_out[y]
    wait_all([wires.send(fin_out.at[ys[d]], fin_ref.at[y], to_y[d]) for d in (2, 1, 3)])
    for i in range(NY):
        out_ref[16 * i : 16 * i + 16, :] = fin_ref[i]
    assert wires.used <= N_WIRES


def body(
    hidden,
    query_down,
    latent_down,
    query_gain,
    latent_gain,
    query_up,
    key_absorb,
    value_absorb,
    out_proj,
    doc_start,
    positions,
):
    half = ROPE // 2
    freqs = 10000.0 ** (-2.0 * np.arange(half) / ROPE)
    freqs = np.broadcast_to(freqs.astype(np.float32)[:, None], (half, 128))
    width = out_proj.shape[1]
    vmem = pltpu.VMEM
    operands = (
        hidden,
        query_down,
        latent_down,
        query_gain,
        latent_gain,
        query_up,
        key_absorb,
        value_absorb,
        out_proj,
        doc_start,
        positions,
        jnp.asarray(freqs),
    )
    scratch = [vmem(a.shape, a.dtype) for a in operands]
    scratch[8] = vmem((NY,) + out_proj.shape, BF16)
    scratch += [
        vmem((1, QRANK), F32),
        vmem((1, LATENT), F32),
        vmem((128, 128), F32),
        vmem((128, 128), F32),
        vmem((3, 128, 256), BF16),
        vmem((3, 128, 256), BF16),
        vmem((3, 128, 384), BF16),
        vmem((3, 128, 384), BF16),
        vmem((128, 256), F32),
        vmem((128, 384), F32),
        vmem((8, 16, 256), BF16),
        vmem((7, 16, 256), BF16),
        vmem((8, 16, 384), BF16),
        vmem((7, 16, 384), BF16),
        vmem((2, 16, 128), F32),
        vmem((2, 3, 16, 128), F32),
        vmem((2, 128, 256), BF16),
        vmem((128, QRANK), BF16),
        vmem((2048, KEY), BF16),
        vmem((512, KEY), BF16),
        vmem((512, 2048), F32),
        vmem((2, 4, 2, 16, 256), BF16),
        vmem((2, 4, 2, 4, 16, 1024), BF16),
        vmem((2, 32, 2 * width), F32),
        vmem((4, 2, 32, 2 * width), BF16),
        vmem((4, 2, 32, 2 * width), BF16),
        vmem((4, 16, width), BF16),
        vmem((4, 16, width), BF16),
        pltpu.SemaphoreType.DMA((len(operands),)),
        pltpu.SemaphoreType.DMA((N_WIRES,)),
        pltpu.SemaphoreType.DMA((N_WIRES,)),
    ]
    return pl.pallas_call(
        kernel,
        out_shape=jax.ShapeDtypeStruct((64, width), BF16),
        in_specs=[pl.BlockSpec(memory_space=pl.ANY)] * len(operands),
        out_specs=pl.BlockSpec(memory_space=pltpu.VMEM),
        scratch_shapes=scratch,
        compiler_params=pltpu.CompilerParams(
            collective_id=0, has_side_effects=True, vmem_limit_bytes=48 * 1024 * 1024
        ),
        name="latent_attention",
    )(*operands)


def solution(mesh):
    in_specs = (
        P("ctx", "head"),
        P("head", None),
        P("head", None),
        P(),
        P(),
        P(None, "head"),
        P(None, "head"),
        P(None, "head"),
        P("head", "ctx"),
        P("ctx"),
        P("ctx"),
    )
    out_specs = P("head", "ctx")
    return jax.shard_map(body, mesh=mesh, in_specs=in_specs, out_specs=out_specs, check_vma=False)
```

```python
import jax
import jax.numpy as jnp
import numpy as np
from jax import lax
from jax.experimental import pallas as pl
from jax.experimental.pallas import tpu as pltpu
from jax.sharding import PartitionSpec as P

LATENT = 512
ROPE = 64
NOPE = 128
VDIM = 128
QRANK = 1536
NX, NY, NZ = 4, 4, 8
KEY = LATENT + 2 * ROPE
SCALE = (NOPE + ROPE) ** (-0.5)
MESH = pl.DeviceIdType.MESH
BF16 = jnp.bfloat16
F32 = jnp.float32
FAR_FIRST = (4, 5, 3, 6, 2, 7, 1)
N_WIRES = 176
VMEM_BYTES = 60 * 1024 * 1024


def dot(a, b):
    return jnp.dot(a, b, preferred_element_type=F32)


def dot_t(a, b):
    return lax.dot_general(a, b, (((1,), (1,)), ((), ())), preferred_element_type=F32)


def rows(start, size):
    return pl.ds(pl.multiple_of(start, size), size)


def ctx_of(x, zh, core):
    return x * 4 + zh * 2 + core


class Wires:
    def __init__(self, send_sems, recv_sems):
        self.send_sems, self.recv_sems, self.used = send_sems, recv_sems, 0

    def send(self, src, dst, to):
        at = self.used
        self.used += 1
        copy = pltpu.make_async_remote_copy(
            src_ref=src,
            dst_ref=dst,
            send_sem=self.send_sems.at[at],
            recv_sem=self.recv_sems.at[at],
            device_id=to,
            device_id_type=MESH,
        )
        copy.start()
        return copy


def wait_all(copies):
    for copy in copies:
        copy.wait()


def kernel(
    hidden_hbm,
    qd_hbm,
    ld_hbm,
    qg_hbm,
    lg_hbm,
    qup_hbm,
    ka_hbm,
    va_hbm,
    wo_hbm,
    doc_hbm,
    pos_hbm,
    freq_hbm,
    out_ref,
    hidden_ref,
    qd_ref,
    ld_ref,
    qg_ref,
    lg_ref,
    qup_ref,
    ka_ref,
    va_ref,
    wo_ref,
    doc_ref,
    pos_ref,
    freq_ref,
    gain_ref,
    lgain_ref,
    cos_ref,
    sin_ref,
    kv_out,
    kv_in,
    q_out,
    q_in,
    kv_own,
    q_own,
    kvz_out,
    kvz_in,
    qz_out,
    qz_in,
    sq_out,
    sq_in,
    kz_ref,
    q_ref,
    k_ref,
    qc_ref,
    s_ref,
    ho_ref,
    g_ref,
    own_ref,
    z_out,
    z_half,
    pair_out,
    z_in,
    fin_out,
    fin_ref,
    load_sems,
    send_sems,
    recv_sems,
):
    ctx = lax.axis_index("ctx")
    head = lax.axis_index("head")
    x, zh, core = ctx // 4, (ctx // 2) % 2, ctx % 2
    y, z = head // NZ, head % NZ
    ys = [lax.rem(y + d, NY) for d in range(NY)]
    zs = [lax.rem(z + d, NZ) for d in range(NZ)]
    other = 1 - zh
    far = ctx_of(x, other, core)
    to_y = [(ctx, ys[d] * NZ + z) for d in range(NY)]
    to_z = [(ctx, y * NZ + zs[d]) for d in range(NZ)]
    to_far = [(far, y * NZ + zs[d]) for d in range(NZ)]
    to_x = [(ctx_of(lax.rem(x + d, NX), zh, core), head) for d in range(NX)]
    to_core = (ctx_of(x, zh, 1 - core), head)
    wires = Wires(send_sems, recv_sems)

    loads = {}
    for i, (name, src, dst) in enumerate(
        [
            ("hidden", hidden_hbm, hidden_ref),
            ("ld", ld_hbm, ld_ref),
            ("qd", qd_hbm, qd_ref),
            ("qg", qg_hbm, qg_ref),
            ("lg", lg_hbm, lg_ref),
            ("pos", pos_hbm, pos_ref),
            ("doc", doc_hbm, doc_ref),
            ("freq", freq_hbm, freq_ref),
            ("qup", qup_hbm, qup_ref),
            ("ka", ka_hbm, ka_ref),
            ("va", va_hbm, va_ref),
            ("wo", wo_hbm, wo_ref.at[y]),
        ]
    ):
        loads[name] = pltpu.make_async_copy(src, dst, load_sems.at[i])
        loads[name].start()
    barrier = pltpu.get_barrier_semaphore()
    partners = to_y[1:] + to_z[1:] + to_far + to_x[1:] + [to_core]
    for to in partners:
        pl.semaphore_signal(barrier, inc=1, device_id=to, device_id_type=MESH)
    pl.semaphore_wait(barrier, len(partners))

    loads["hidden"].wait()
    loads["ld"].wait()
    hid = hidden_ref[...].T
    rot = dot(hid, ld_ref[:, LATENT:])
    rot = jnp.concatenate([rot, jnp.zeros_like(rot)], axis=1)
    kv_y = []
    for d in (2, 1, 3):
        kv_out[d - 1, :, 0:128] = dot(hid, ld_ref[:, rows(ys[d] * 128, 128)]).astype(BF16)
        kv_out[d - 1, :, 128:256] = rot.astype(BF16)
        kv_y.append(wires.send(kv_out.at[d - 1], kv_in.at[d - 1], to_y[d]))
    l_cols = rows(y * 128, 128)
    q_cols = rows(y * 384, 384)
    kv_own[:, 0:128] = dot(hid, ld_ref[:, l_cols])
    kv_own[:, 128:256] = rot
    loads["qd"].wait()
    for d in (2, 1, 3):
        q_out[d - 1] = dot(hid, qd_ref[:, rows(ys[d] * 384, 384)]).astype(BF16)
    q_own[...] = dot(hid, qd_ref[:, q_cols])

    def over_y(copies, own, received):
        wait_all(copies)
        total = own[...]
        for d in range(NY - 1):
            total = total + received[d].astype(F32)
        own[...] = total
        return total

    def to_all_z(total, out, received):
        for i in range(NZ):
            out[i] = total[16 * i : 16 * i + 16].astype(BF16)
        return [wires.send(out.at[zs[d]], received.at[d - 1], to_z[d]) for d in FAR_FIRST]

    here = rows(z * 16, 16)

    def over_z(copies, own, received):
        wait_all(copies)
        total = own[here, :]
        for d in range(NZ - 1):
            total = total + received[d].astype(F32)
        return total

    def square(i, values):
        total = jnp.sum(values * values, axis=1, keepdims=True)
        sq_out[i] = jnp.broadcast_to(total, (16, 128))
        return [wires.send(sq_out.at[i], sq_in.at[i, d - 1], to_y[d]) for d in (2, 1, 3)]

    def scale_of(i, copies, count):
        wait_all(copies)
        total = sq_out[i] + sq_in[i, 0] + sq_in[i, 1] + sq_in[i, 2]
        return lax.rsqrt(total[:, 0:1] / count + 1e-06)

    kv_z = to_all_z(over_y(kv_y, kv_own, kv_in), kvz_out, kvz_in)
    q_y = [wires.send(q_out.at[d - 1], q_in.at[d - 1], to_y[d]) for d in (2, 1, 3)]
    loads["pos"].wait()
    loads["freq"].wait()
    freq = jnp.broadcast_to(freq_ref[...][None, :], (128, 128)).T[: ROPE // 2]
    angles = freq * pos_ref[...].astype(F32)[None, :]
    cosine, sine = jnp.cos(angles), jnp.sin(angles)
    cos_ref[...] = jnp.concatenate([cosine, cosine, cosine, cosine], axis=0).T
    sin_ref[...] = jnp.concatenate([-sine, sine, -sine, sine], axis=0).T
    loads["qg"].wait()
    loads["lg"].wait()
    gain_ref[...] = qg_ref[...][None, :]
    lgain_ref[...] = lg_ref[...][None, :]

    mine = over_z(kv_z, kv_own, kvz_in)
    lat, rot = mine[:, :128], mine[:, 128:]
    kv_sq = square(0, lat)
    half = ROPE // 2
    swapped = jnp.concatenate([rot[:, half:ROPE], rot[:, :half]], axis=1)
    turned = rot[:, :ROPE] * cos_ref[here, :ROPE] + swapped * sin_ref[here, :ROPE]
    kz_ref[zh, here, 128:256] = jnp.concatenate([turned, jnp.zeros_like(turned)], axis=1).astype(BF16)
    q_total = over_y(q_y, q_own, q_in)
    l_scale = scale_of(0, kv_sq, LATENT)
    kz_ref[zh, here, 0:128] = (lat * l_scale * lgain_ref[:, l_cols]).astype(BF16)
    piece = kz_ref.at[zh, here]
    kz = [wires.send(piece, piece, to_z[d]) for d in FAR_FIRST]
    kz += [wires.send(piece, piece, to_far[d]) for d in range(NZ)]
    q_z = to_all_z(q_total, qz_out, qz_in)

    def key_rows(d, i):
        return rows(ctx_of(lax.rem(x + NX - d, NX), i, core) * 128, 128)

    wait_all(kz)
    for i in range(2):
        k_ref[key_rows(0, i), l_cols] = kz_ref[i, :, 0:128]
        k_ref[key_rows(0, i), LATENT:KEY] = kz_ref[i, :, 128:256]

    def key_over_y(d, i):
        piece = k_ref.at[key_rows(d, i), l_cols]
        return [wires.send(piece, piece, to_y[e]) for e in (2, 1, 3)]

    first_y = key_over_y(0, 0)
    second_x, second_y = {}, {}
    for d in (2, 1, 3):
        second_x[d] = []
        for cols in (l_cols, pl.ds(LATENT, 128)):
            piece = k_ref.at[key_rows(0, 1), cols]
            second_x[d].append(wires.send(piece, piece, to_x[d]))
    second_y[0] = key_over_y(0, 1)
    q_low = over_z(q_z, q_own, qz_in)
    q_sq = square(1, q_low)
    wait_all(first_y)
    first_x = {}
    for d in (2, 1, 3):
        piece = k_ref.at[key_rows(0, 0), :]
        first_x[d] = [wires.send(piece, piece, to_x[d])]
    q_scale = scale_of(1, q_sq, QRANK)
    q_ref[here, q_cols] = (q_low * q_scale * gain_ref[:, q_cols]).astype(BF16)
    piece = q_ref.at[here, q_cols]
    qz = [wires.send(piece, piece, to_z[d]) for d in FAR_FIRST]
    for d in (1, 3, 2):
        wait_all(second_x[d])
        second_y[d] = key_over_y(d, 1)
    wait_all(qz)
    piece = q_ref.at[:, q_cols]
    q_all = [wires.send(piece, piece, to_y[d]) for d in (2, 1, 3)]

    key_core = {}

    def key_to_core(d):
        if d:
            wait_all(first_x[d])
        wait_all(second_y[d])
        key_core[d] = []
        for i in range(2):
            piece = k_ref.at[key_rows(d, i), :]
            key_core[d].append(wires.send(piece, piece, to_core))

    for name in ("qup", "ka", "va", "doc"):
        loads[name].wait()
    key_to_core(0)
    wait_all(q_all)
    full = dot(q_ref[...], qup_ref[...])
    cosine, sine = cos_ref[:, :ROPE], sin_ref[:, :ROPE]
    for h in range(4):
        at = h * (NOPE + ROPE)
        nope = full[:, at : at + NOPE].astype(BF16)
        raw = full[:, at + NOPE : at + NOPE + ROPE]
        swapped = jnp.concatenate([raw[:, half:], raw[:, :half]], axis=1)
        turned = raw * cosine + swapped * sine
        low = dot_t(nope, ka_ref[:, h * NOPE : (h + 1) * NOPE])
        mine = slice(h * 128, h * 128 + 128)
        qc_ref[mine, :LATENT] = low.astype(BF16)
        qc_ref[mine, LATENT:] = jnp.concatenate([turned, jnp.zeros_like(turned)], axis=1).astype(BF16)

    doc = jnp.broadcast_to(doc_ref[...].astype(F32)[None, :], (128, 128)).T[:, 0:1].astype(jnp.int32)
    query_index = ctx * 128 + lax.broadcasted_iota(jnp.int32, (128, 512), 0)
    key_lane = lax.broadcasted_iota(jnp.int32, (128, 512), 1)
    top = [None] * 4

    def scores(d):
        wait_all(key_core[d])
        at = rows(lax.rem(x + NX - d, NX) * 512, 512)
        key_index = key_lane + lax.rem(x + NX - d, NX) * 512
        bias = jnp.where((key_index <= query_index) & (key_index >= doc), 0.0, -1e30)
        block = dot_t(qc_ref[...], k_ref[at, :])
        for h in range(4):
            mine = slice(h * 128, h * 128 + 128)
            values = block[mine] * SCALE + bias
            s_ref[mine, at] = values
            most = jnp.max(values, axis=1, keepdims=True)
            top[h] = most if top[h] is None else jnp.maximum(top[h], most)

    key_to_core(1)
    scores(0)
    key_to_core(3)
    scores(1)
    key_to_core(2)
    loads["wo"].wait()
    weights = [wires.send(wo_ref.at[y], wo_ref.at[y], to_y[d]) for d in (2, 1, 3)]
    scores(3)
    scores(2)

    here_zc, far_zc = zh * 2 + core, other * 2 + core
    cols = rows(y * 256, 256)

    def mix(pair):
        mine = slice(pair * 256, pair * 256 + 256)
        most = jnp.concatenate([top[2 * pair], top[2 * pair + 1]], axis=0)
        weighted = jnp.zeros((256, LATENT), F32)
        total = jnp.zeros((256, 1), F32)
        for j in range(4):
            expo = jnp.exp(s_ref[mine, 512 * j : 512 * j + 512] - most)
            total = total + jnp.sum(expo, axis=1, keepdims=True)
            weighted = weighted + dot(expo.astype(BF16), k_ref[512 * j : 512 * j + 512, :LATENT])
        mixed = (weighted / total).astype(BF16)
        for i in range(2):
            at = (2 * pair + i) * VDIM
            result = dot(mixed[128 * i : 128 * i + 128], va_ref[:, at : at + VDIM]).astype(BF16)
            for part in range(4):
                for side in range(2):
                    first = 64 * side + 16 * part
                    ho_ref[pair, part, side, :, 128 * i : 128 * i + 128] = result[first : first + 16]
        g_ref[pair, here_zc, :, x, :, cols] = ho_ref[pair, y]
        spot = g_ref.at[pair, here_zc, :, x, :, cols]
        return [wires.send(ho_ref.at[pair, ys[d]], spot, to_y[d]) for d in (2, 1, 3)]

    def block(pair, zc, d):
        return g_ref.at[pair, zc, :, lax.rem(x + NX - d, NX)]

    def spread(pair, zc, over_x):
        piece = block(pair, zc, 0)
        for d in (2, 1, 3):
            over_x[pair, zc is far_zc, d] = wires.send(piece, piece, to_x[d])
        return wires.send(piece, piece, to_core)

    over_x, over_core, over_far = {}, [], {}

    def launch(pair, copies):
        wait_all(copies)
        piece = block(pair, here_zc, 0)
        if pair:
            over_far[0].wait_send()
        over_far[pair] = wires.send(piece, piece, to_far[0])
        over_core.append(spread(pair, here_zc, over_x))

    handed = mix(0)
    second = mix(1)
    launch(0, handed)
    launch(1, second)
    for pair in range(2):
        if pair:
            over_far[pair].wait_send()
        over_far[pair].wait_recv()
        over_core.append(spread(pair, far_zc, over_x))
    for pair in range(2):
        for zc in (here_zc, far_zc):
            for d in (1, 3, 2):
                over_x[pair, zc is far_zc, d].wait()
                piece = block(pair, zc, d)
                over_core.append(wires.send(piece, piece, to_core))
    wait_all(over_core)
    wait_all(weights)

    pair_at, odd = z // 2, z % 2
    near = (ctx, y * NZ + pair_at * 2 + 1 - odd)
    halves, sums = {}, {}
    for k in (2, 1, 3, 0):
        zc = lax.rem(pair_at + k, 4)
        total = jnp.zeros((128, out_ref.shape[1]), F32)
        for pair in range(2):
            tokens = g_ref[pair, zc].reshape(128, 1024)
            for i in range(NY):
                total = total + dot_t(
                    tokens[:, 256 * i : 256 * i + 256], wo_ref[i, :, 256 * pair : 256 * pair + 256]
                )
        for side in range(2):
            part = total[64 * side : 64 * side + 64]
            part = jnp.concatenate([part[:32], part[32:]], axis=1)
            own_ref[k, side] = part
            z_out[k, side] = part.astype(BF16)
        halves[k] = wires.send(z_out.at[k, 1 - odd], z_half.at[k], near)
    for k in (2, 1, 3):
        halves[k].wait()
        pair_out[k] = (own_ref[k, odd] + z_half[k].astype(F32)).astype(BF16)
        to = (ctx, y * NZ + lax.rem(pair_at + k, 4) * 2 + odd)
        sums[k] = wires.send(pair_out.at[k], z_in.at[k], to)
    halves[0].wait()
    total = own_ref[0, odd] + z_half[0].astype(F32)
    for k in (1, 3, 2):
        sums[k].wait()
        total = total + z_in[k].astype(F32)
    width = out_ref.shape[1]
    result = jnp.concatenate([total[:, :width], total[:, width:]], axis=0).astype(BF16)
    for i in range(NX):
        fin_out[i] = result[16 * i : 16 * i + 16]
    fin_ref[y] = fin_out[y]
    wait_all([wires.send(fin_out.at[ys[d]], fin_ref.at[y], to_y[d]) for d in (2, 1, 3)])
    for i in range(NY):
        out_ref[16 * i : 16 * i + 16, :] = fin_ref[i]
    assert wires.used <= N_WIRES


def body(
    hidden,
    query_down,
    latent_down,
    query_gain,
    latent_gain,
    query_up,
    key_absorb,
    value_absorb,
    out_proj,
    doc_start,
    positions,
):
    half = ROPE // 2
    freqs = np.zeros((128,), np.float32)
    freqs[:half] = 10000.0 ** (-2.0 * np.arange(half) / ROPE)
    width = out_proj.shape[1]
    hidden, out_proj = hidden.T, out_proj.T
    vmem = pltpu.VMEM
    operands = (
        hidden,
        query_down,
        latent_down,
        query_gain,
        latent_gain,
        query_up,
        key_absorb,
        value_absorb,
        out_proj,
        doc_start,
        positions,
        jnp.asarray(freqs),
    )
    scratch = [vmem(a.shape, a.dtype) for a in operands]
    scratch[8] = vmem((NY,) + out_proj.shape, BF16)
    scratch += [
        vmem((1, QRANK), F32),
        vmem((1, LATENT), F32),
        vmem((128, 128), F32),
        vmem((128, 128), F32),
        vmem((3, 128, 256), BF16),
        vmem((3, 128, 256), BF16),
        vmem((3, 128, 384), BF16),
        vmem((3, 128, 384), BF16),
        vmem((128, 256), F32),
        vmem((128, 384), F32),
        vmem((8, 16, 256), BF16),
        vmem((7, 16, 256), BF16),
        vmem((8, 16, 384), BF16),
        vmem((7, 16, 384), BF16),
        vmem((2, 16, 128), F32),
        vmem((2, 3, 16, 128), F32),
        vmem((2, 128, 256), BF16),
        vmem((128, QRANK), BF16),
        vmem((2048, KEY), BF16),
        vmem((512, KEY), BF16),
        vmem((512, 2048), F32),
        vmem((2, 4, 2, 16, 256), BF16),
        vmem((2, 4, 2, 4, 16, 1024), BF16),
        vmem((4, 2, 32, 2 * width), F32),
        vmem((4, 2, 32, 2 * width), BF16),
        vmem((4, 32, 2 * width), BF16),
        vmem((4, 32, 2 * width), BF16),
        vmem((4, 32, 2 * width), BF16),
        vmem((4, 16, width), BF16),
        vmem((4, 16, width), BF16),
        pltpu.SemaphoreType.DMA((len(operands),)),
        pltpu.SemaphoreType.DMA((N_WIRES,)),
        pltpu.SemaphoreType.DMA((N_WIRES,)),
    ]
    return pl.pallas_call(
        kernel,
        out_shape=jax.ShapeDtypeStruct((64, width), BF16),
        in_specs=[pl.BlockSpec(memory_space=pl.ANY)] * len(operands),
        out_specs=pl.BlockSpec(memory_space=pltpu.VMEM),
        scratch_shapes=scratch,
        compiler_params=pltpu.CompilerParams(
            collective_id=0, has_side_effects=True, vmem_limit_bytes=VMEM_BYTES
        ),
        name="latent_attention",
    )(*operands)


def solution(mesh):
    in_specs = (
        P("ctx", "head"),
        P("head", None),
        P("head", None),
        P(),
        P(),
        P(None, "head"),
        P(None, "head"),
        P(None, "head"),
        P("head", "ctx"),
        P("ctx"),
        P("ctx"),
    )
    out_specs = P("head", "ctx")
    return jax.shard_map(body, mesh=mesh, in_specs=in_specs, out_specs=out_specs, check_vma=False)
```

```python
import jax
import jax.numpy as jnp
import numpy as np
from jax import lax
from jax.experimental import pallas as pl
from jax.experimental.pallas import tpu as pltpu
from jax.sharding import PartitionSpec as P

LATENT = 512
ROPE = 64
NOPE = 128
VDIM = 128
QRANK = 1536
NX, NY, NZ = 4, 4, 8
KEY = LATENT + 2 * ROPE
SCALE = (NOPE + ROPE) ** (-0.5)
MESH = pl.DeviceIdType.MESH
BF16 = jnp.bfloat16
F32 = jnp.float32
FAR_FIRST = (4, 5, 3, 6, 2, 7, 1)
N_WIRES = 176
VMEM_BYTES = 60 * 1024 * 1024


def dot(a, b):
    return jnp.dot(a, b, preferred_element_type=F32)


def dot_t(a, b):
    return lax.dot_general(a, b, (((1,), (1,)), ((), ())), preferred_element_type=F32)


def rows(start, size):
    return pl.ds(pl.multiple_of(start, size), size)


def ctx_of(x, zh, core):
    return x * 4 + zh * 2 + core


class Wires:
    def __init__(self, send_sems, recv_sems):
        self.send_sems, self.recv_sems, self.used = send_sems, recv_sems, 0

    def send(self, src, dst, to):
        at = self.used
        self.used += 1
        copy = pltpu.make_async_remote_copy(
            src_ref=src,
            dst_ref=dst,
            send_sem=self.send_sems.at[at],
            recv_sem=self.recv_sems.at[at],
            device_id=to,
            device_id_type=MESH,
        )
        copy.start()
        return copy


def wait_all(copies):
    for copy in copies:
        copy.wait()


def kernel(
    hidden_hbm,
    qd_hbm,
    ld_hbm,
    qg_hbm,
    lg_hbm,
    qup_hbm,
    ka_hbm,
    va_hbm,
    wo_hbm,
    doc_hbm,
    pos_hbm,
    freq_hbm,
    out_ref,
    hidden_ref,
    qd_ref,
    ld_ref,
    qg_ref,
    lg_ref,
    qup_ref,
    ka_ref,
    va_ref,
    wo_ref,
    doc_ref,
    pos_ref,
    freq_ref,
    gain_ref,
    lgain_ref,
    cos_ref,
    sin_ref,
    kv_out,
    kv_in,
    q_out,
    q_in,
    kv_own,
    q_own,
    kvz_out,
    kvz_in,
    qz_out,
    qz_in,
    sq_out,
    sq_in,
    kz_ref,
    q_ref,
    k_ref,
    qc_ref,
    s_ref,
    ho_ref,
    g_ref,
    own_ref,
    z_out,
    z_half,
    pair_out,
    z_in,
    fin_out,
    fin_ref,
    load_sems,
    send_sems,
    recv_sems,
):
    ctx = lax.axis_index("ctx")
    head = lax.axis_index("head")
    x, zh, core = ctx // 4, (ctx // 2) % 2, ctx % 2
    y, z = head // NZ, head % NZ
    ys = [lax.rem(y + d, NY) for d in range(NY)]
    zs = [lax.rem(z + d, NZ) for d in range(NZ)]
    other = 1 - zh
    far = ctx_of(x, other, core)
    to_y = [(ctx, ys[d] * NZ + z) for d in range(NY)]
    to_z = [(ctx, y * NZ + zs[d]) for d in range(NZ)]
    to_far = [(far, y * NZ + zs[d]) for d in range(NZ)]
    to_x = [(ctx_of(lax.rem(x + d, NX), zh, core), head) for d in range(NX)]
    to_core = (ctx_of(x, zh, 1 - core), head)
    wires = Wires(send_sems, recv_sems)

    loads = {}
    for i, (name, src, dst) in enumerate(
        [
            ("hidden", hidden_hbm, hidden_ref),
            ("ld", ld_hbm, ld_ref),
            ("qd", qd_hbm, qd_ref),
            ("qg", qg_hbm, qg_ref),
            ("lg", lg_hbm, lg_ref),
            ("pos", pos_hbm, pos_ref),
            ("doc", doc_hbm, doc_ref),
            ("freq", freq_hbm, freq_ref),
            ("qup", qup_hbm, qup_ref),
            ("ka", ka_hbm, ka_ref),
            ("va", va_hbm, va_ref),
            ("wo", wo_hbm, wo_ref.at[y]),
        ]
    ):
        loads[name] = pltpu.make_async_copy(src, dst, load_sems.at[i])
        loads[name].start()
    barrier = pltpu.get_barrier_semaphore()
    partners = to_y[1:] + to_z[1:] + to_far + to_x[1:] + [to_core]
    for to in partners:
        pl.semaphore_signal(barrier, inc=1, device_id=to, device_id_type=MESH)
    pl.semaphore_wait(barrier, len(partners))

    loads["hidden"].wait()
    loads["ld"].wait()
    hid = hidden_ref[...].T
    rot = dot(hid, ld_ref[:, LATENT:])
    rot = jnp.concatenate([rot, jnp.zeros_like(rot)], axis=1)
    kv_y = []
    for d in (2, 1, 3):
        kv_out[d - 1, :, 0:128] = dot(hid, ld_ref[:, rows(ys[d] * 128, 128)]).astype(BF16)
        kv_out[d - 1, :, 128:256] = rot.astype(BF16)
        kv_y.append(wires.send(kv_out.at[d - 1], kv_in.at[d - 1], to_y[d]))
    l_cols = rows(y * 128, 128)
    q_cols = rows(y * 384, 384)
    kv_own[:, 0:128] = dot(hid, ld_ref[:, l_cols])
    kv_own[:, 128:256] = rot
    loads["qd"].wait()
    for d in (2, 1, 3):
        q_out[d - 1] = dot(hid, qd_ref[:, rows(ys[d] * 384, 384)]).astype(BF16)
    q_own[...] = dot(hid, qd_ref[:, q_cols])

    def over_y(copies, own, received):
        wait_all(copies)
        total = own[...]
        for d in range(NY - 1):
            total = total + received[d].astype(F32)
        own[...] = total
        return total

    def to_all_z(total, out, received):
        for i in range(NZ):
            out[i] = total[16 * i : 16 * i + 16].astype(BF16)
        return [wires.send(out.at[zs[d]], received.at[d - 1], to_z[d]) for d in FAR_FIRST]

    here = rows(z * 16, 16)

    def over_z(copies, own, received):
        wait_all(copies)
        total = own[here, :]
        for d in range(NZ - 1):
            total = total + received[d].astype(F32)
        return total

    def square(i, values):
        total = jnp.sum(values * values, axis=1, keepdims=True)
        sq_out[i] = jnp.broadcast_to(total, (16, 128))
        return [wires.send(sq_out.at[i], sq_in.at[i, d - 1], to_y[d]) for d in (2, 1, 3)]

    def scale_of(i, copies, count):
        wait_all(copies)
        total = sq_out[i] + sq_in[i, 0] + sq_in[i, 1] + sq_in[i, 2]
        return lax.rsqrt(total[:, 0:1] / count + 1e-06)

    kv_z = to_all_z(over_y(kv_y, kv_own, kv_in), kvz_out, kvz_in)
    q_y = [wires.send(q_out.at[d - 1], q_in.at[d - 1], to_y[d]) for d in (2, 1, 3)]
    loads["pos"].wait()
    loads["freq"].wait()
    freq = jnp.broadcast_to(freq_ref[...][None, :], (128, 128)).T[: ROPE // 2]
    angles = freq * pos_ref[...].astype(F32)[None, :]
    cosine, sine = jnp.cos(angles), jnp.sin(angles)
    cos_ref[...] = jnp.concatenate([cosine, cosine, cosine, cosine], axis=0).T
    sin_ref[...] = jnp.concatenate([-sine, sine, -sine, sine], axis=0).T
    loads["qg"].wait()
    loads["lg"].wait()
    gain_ref[...] = qg_ref[...][None, :]
    lgain_ref[...] = lg_ref[...][None, :]

    mine = over_z(kv_z, kv_own, kvz_in)
    lat, rot = mine[:, :128], mine[:, 128:]
    kv_sq = square(0, lat)
    half = ROPE // 2
    swapped = jnp.concatenate([rot[:, half:ROPE], rot[:, :half]], axis=1)
    turned = rot[:, :ROPE] * cos_ref[here, :ROPE] + swapped * sin_ref[here, :ROPE]
    kz_ref[zh, here, 128:256] = jnp.concatenate([turned, jnp.zeros_like(turned)], axis=1).astype(BF16)
    q_total = over_y(q_y, q_own, q_in)
    l_scale = scale_of(0, kv_sq, LATENT)
    kz_ref[zh, here, 0:128] = (lat * l_scale * lgain_ref[:, l_cols]).astype(BF16)
    piece = kz_ref.at[zh, here]
    kz = [wires.send(piece, piece, to_z[d]) for d in FAR_FIRST]
    kz += [wires.send(piece, piece, to_far[d]) for d in range(NZ)]
    q_z = to_all_z(q_total, qz_out, qz_in)
    loads["wo"].wait()
    weights = []

    def share_weights(i):
        size = wo_ref.shape[1] // 4
        piece = wo_ref.at[y, i * size : i * size + size, :]
        weights.extend(wires.send(piece, piece, to_y[d]) for d in (2, 1, 3))

    share_weights(0)

    def key_rows(d, i):
        return rows(ctx_of(lax.rem(x + NX - d, NX), i, core) * 128, 128)

    wait_all(kz)
    for i in range(2):
        k_ref[key_rows(0, i), l_cols] = kz_ref[i, :, 0:128]
        k_ref[key_rows(0, i), LATENT:KEY] = kz_ref[i, :, 128:256]

    def key_over_y(d, i):
        piece = k_ref.at[key_rows(d, i), l_cols]
        return [wires.send(piece, piece, to_y[e]) for e in (2, 1, 3)]

    first_y = key_over_y(0, 0)
    second_x, second_y = {}, {}
    for d in (2, 1, 3):
        second_x[d] = []
        for cols in (l_cols, pl.ds(LATENT, 128)):
            piece = k_ref.at[key_rows(0, 1), cols]
            second_x[d].append(wires.send(piece, piece, to_x[d]))
    second_y[0] = key_over_y(0, 1)
    q_low = over_z(q_z, q_own, qz_in)
    q_sq = square(1, q_low)
    wait_all(first_y)
    first_x = {}
    for d in (2, 1, 3):
        piece = k_ref.at[key_rows(0, 0), :]
        first_x[d] = [wires.send(piece, piece, to_x[d])]
    q_scale = scale_of(1, q_sq, QRANK)
    q_ref[here, q_cols] = (q_low * q_scale * gain_ref[:, q_cols]).astype(BF16)
    piece = q_ref.at[here, q_cols]
    qz = [wires.send(piece, piece, to_z[d]) for d in FAR_FIRST]
    for d in (1, 3, 2):
        wait_all(second_x[d])
        second_y[d] = key_over_y(d, 1)
    wait_all(qz)
    piece = q_ref.at[:, q_cols]
    q_all = [wires.send(piece, piece, to_y[d]) for d in (2, 1, 3)]

    key_core = {}

    def key_to_core(d):
        if d:
            wait_all(first_x[d])
        wait_all(second_y[d])
        key_core[d] = []
        for i in range(2):
            piece = k_ref.at[key_rows(d, i), :]
            key_core[d].append(wires.send(piece, piece, to_core))

    for name in ("qup", "ka", "va", "doc"):
        loads[name].wait()
    key_to_core(0)
    wait_all(q_all)
    share_weights(1)
    full = dot(q_ref[...], qup_ref[...])
    cosine, sine = cos_ref[:, :ROPE], sin_ref[:, :ROPE]
    for h in range(4):
        at = h * (NOPE + ROPE)
        nope = full[:, at : at + NOPE].astype(BF16)
        raw = full[:, at + NOPE : at + NOPE + ROPE]
        swapped = jnp.concatenate([raw[:, half:], raw[:, :half]], axis=1)
        turned = raw * cosine + swapped * sine
        low = dot_t(nope, ka_ref[:, h * NOPE : (h + 1) * NOPE])
        mine = slice(h * 128, h * 128 + 128)
        qc_ref[mine, :LATENT] = low.astype(BF16)
        qc_ref[mine, LATENT:] = jnp.concatenate([turned, jnp.zeros_like(turned)], axis=1).astype(BF16)

    doc = jnp.broadcast_to(doc_ref[...].astype(F32)[None, :], (128, 128)).T[:, 0:1].astype(jnp.int32)
    query_index = ctx * 128 + lax.broadcasted_iota(jnp.int32, (128, 512), 0)
    key_lane = lax.broadcasted_iota(jnp.int32, (128, 512), 1)
    top = [None] * 4

    def scores(d):
        wait_all(key_core[d])
        at = rows(lax.rem(x + NX - d, NX) * 512, 512)
        key_index = key_lane + lax.rem(x + NX - d, NX) * 512
        bias = jnp.where((key_index <= query_index) & (key_index >= doc), 0.0, -1e30)
        block = dot_t(qc_ref[...], k_ref[at, :])
        for h in range(4):
            mine = slice(h * 128, h * 128 + 128)
            values = block[mine] * SCALE + bias
            s_ref[mine, at] = values
            most = jnp.max(values, axis=1, keepdims=True)
            top[h] = most if top[h] is None else jnp.maximum(top[h], most)

    key_to_core(1)
    scores(0)
    key_to_core(3)
    scores(1)
    key_to_core(2)
    scores(3)
    scores(2)

    here_zc, far_zc = zh * 2 + core, other * 2 + core
    cols = rows(y * 256, 256)

    def mix(pair, between):
        mine = slice(pair * 256, pair * 256 + 256)
        most = jnp.concatenate([top[2 * pair], top[2 * pair + 1]], axis=0)
        weighted = jnp.zeros((256, LATENT), F32)
        total = jnp.zeros((256, 1), F32)
        for j in range(4):
            expo = jnp.exp(s_ref[mine, 512 * j : 512 * j + 512] - most)
            total = total + jnp.sum(expo, axis=1, keepdims=True)
            weighted = weighted + dot(expo.astype(BF16), k_ref[512 * j : 512 * j + 512, :LATENT])
        between()
        mixed = (weighted / total).astype(BF16)
        for i in range(2):
            at = (2 * pair + i) * VDIM
            result = dot(mixed[128 * i : 128 * i + 128], va_ref[:, at : at + VDIM]).astype(BF16)
            for part in range(4):
                for side in range(2):
                    first = 64 * side + 16 * part
                    ho_ref[pair, part, side, :, 128 * i : 128 * i + 128] = result[first : first + 16]
        g_ref[pair, here_zc, :, x, :, cols] = ho_ref[pair, y]
        spot = g_ref.at[pair, here_zc, :, x, :, cols]
        return [wires.send(ho_ref.at[pair, ys[d]], spot, to_y[d]) for d in (2, 1, 3)]

    def block(pair, zc, d):
        return g_ref.at[pair, zc, :, lax.rem(x + NX - d, NX)]

    def spread(pair, zc, over_x):
        piece = block(pair, zc, 0)
        for d in (2, 1, 3):
            over_x[pair, zc is far_zc, d] = wires.send(piece, piece, to_x[d])
        return wires.send(piece, piece, to_core)

    over_x, over_core, over_far = {}, [], {}

    def launch(pair, copies):
        wait_all(copies)
        piece = block(pair, here_zc, 0)
        if pair:
            over_far[0].wait_send()
        over_far[pair] = wires.send(piece, piece, to_far[0])
        over_core.append(spread(pair, here_zc, over_x))

    handed = mix(0, lambda: None)
    second = mix(1, lambda: launch(0, handed))
    launch(1, second)
    share_weights(2)
    share_weights(3)
    for pair in range(2):
        if pair:
            over_far[pair].wait_send()
        over_far[pair].wait_recv()
        over_core.append(spread(pair, far_zc, over_x))
    for pair in range(2):
        for zc in (here_zc, far_zc):
            for d in (1, 3, 2):
                over_x[pair, zc is far_zc, d].wait()
                piece = block(pair, zc, d)
                over_core.append(wires.send(piece, piece, to_core))
    wait_all(over_core)
    wait_all(weights)

    pair_at, odd = z // 2, z % 2
    near = (ctx, y * NZ + pair_at * 2 + 1 - odd)
    halves, sums = {}, {}
    for k in (2, 1, 3, 0):
        zc = lax.rem(pair_at + k, 4)
        total = jnp.zeros((128, out_ref.shape[1]), F32)
        for pair in range(2):
            tokens = g_ref[pair, zc].reshape(128, 1024)
            for i in range(NY):
                total = total + dot_t(
                    tokens[:, 256 * i : 256 * i + 256], wo_ref[i, :, 256 * pair : 256 * pair + 256]
                )
        for side in range(2):
            part = total[64 * side : 64 * side + 64]
            part = jnp.concatenate([part[:32], part[32:]], axis=1)
            own_ref[k, side] = part
            z_out[k, side] = part.astype(BF16)
        halves[k] = wires.send(z_out.at[k, 1 - odd], z_half.at[k], near)
    for k in (2, 1, 3):
        halves[k].wait()
        pair_out[k] = (own_ref[k, odd] + z_half[k].astype(F32)).astype(BF16)
        to = (ctx, y * NZ + lax.rem(pair_at + k, 4) * 2 + odd)
        sums[k] = wires.send(pair_out.at[k], z_in.at[k], to)
    halves[0].wait()
    total = own_ref[0, odd] + z_half[0].astype(F32)
    for k in (1, 3, 2):
        sums[k].wait()
        total = total + z_in[k].astype(F32)
    width = out_ref.shape[1]
    result = jnp.concatenate([total[:, :width], total[:, width:]], axis=0).astype(BF16)
    for i in range(NX):
        fin_out[i] = result[16 * i : 16 * i + 16]
    fin_ref[y] = fin_out[y]
    wait_all([wires.send(fin_out.at[ys[d]], fin_ref.at[y], to_y[d]) for d in (2, 1, 3)])
    for i in range(NY):
        out_ref[16 * i : 16 * i + 16, :] = fin_ref[i]
    assert wires.used <= N_WIRES


def body(
    hidden,
    query_down,
    latent_down,
    query_gain,
    latent_gain,
    query_up,
    key_absorb,
    value_absorb,
    out_proj,
    doc_start,
    positions,
):
    half = ROPE // 2
    freqs = np.zeros((128,), np.float32)
    freqs[:half] = 10000.0 ** (-2.0 * np.arange(half) / ROPE)
    width = out_proj.shape[1]
    hidden, out_proj = hidden.T, out_proj.T
    vmem = pltpu.VMEM
    operands = (
        hidden,
        query_down,
        latent_down,
        query_gain,
        latent_gain,
        query_up,
        key_absorb,
        value_absorb,
        out_proj,
        doc_start,
        positions,
        jnp.asarray(freqs),
    )
    scratch = [vmem(a.shape, a.dtype) for a in operands]
    scratch[8] = vmem((NY,) + out_proj.shape, BF16)
    scratch += [
        vmem((1, QRANK), F32),
        vmem((1, LATENT), F32),
        vmem((128, 128), F32),
        vmem((128, 128), F32),
        vmem((3, 128, 256), BF16),
        vmem((3, 128, 256), BF16),
        vmem((3, 128, 384), BF16),
        vmem((3, 128, 384), BF16),
        vmem((128, 256), F32),
        vmem((128, 384), F32),
        vmem((8, 16, 256), BF16),
        vmem((7, 16, 256), BF16),
        vmem((8, 16, 384), BF16),
        vmem((7, 16, 384), BF16),
        vmem((2, 16, 128), F32),
        vmem((2, 3, 16, 128), F32),
        vmem((2, 128, 256), BF16),
        vmem((128, QRANK), BF16),
        vmem((2048, KEY), BF16),
        vmem((512, KEY), BF16),
        vmem((512, 2048), F32),
        vmem((2, 4, 2, 16, 256), BF16),
        vmem((2, 4, 2, 4, 16, 1024), BF16),
        vmem((4, 2, 32, 2 * width), F32),
        vmem((4, 2, 32, 2 * width), BF16),
        vmem((4, 32, 2 * width), BF16),
        vmem((4, 32, 2 * width), BF16),
        vmem((4, 32, 2 * width), BF16),
        vmem((4, 16, width), BF16),
        vmem((4, 16, width), BF16),
        pltpu.SemaphoreType.DMA((len(operands),)),
        pltpu.SemaphoreType.DMA((N_WIRES,)),
        pltpu.SemaphoreType.DMA((N_WIRES,)),
    ]
    return pl.pallas_call(
        kernel,
        out_shape=jax.ShapeDtypeStruct((64, width), BF16),
        in_specs=[pl.BlockSpec(memory_space=pl.ANY)] * len(operands),
        out_specs=pl.BlockSpec(memory_space=pltpu.VMEM),
        scratch_shapes=scratch,
        compiler_params=pltpu.CompilerParams(
            collective_id=0, has_side_effects=True, vmem_limit_bytes=VMEM_BYTES
        ),
        name="latent_attention",
    )(*operands)


def solution(mesh):
    in_specs = (
        P("ctx", "head"),
        P("head", None),
        P("head", None),
        P(),
        P(),
        P(None, "head"),
        P(None, "head"),
        P(None, "head"),
        P("head", "ctx"),
        P("ctx"),
        P("ctx"),
    )
    out_specs = P("head", "ctx")
    return jax.shard_map(body, mesh=mesh, in_specs=in_specs, out_specs=out_specs, check_vma=False)
```

```python
import jax
import jax.numpy as jnp
import numpy as np
from jax import lax
from jax.experimental import pallas as pl
from jax.experimental.pallas import tpu as pltpu
from jax.sharding import PartitionSpec as P

LATENT = 512
ROPE = 64
NOPE = 128
VDIM = 128
QRANK = 1536
NX, NY, NZ = 4, 4, 8
KEY = LATENT + 2 * ROPE
SCALE = (NOPE + ROPE) ** (-0.5)
MESH = pl.DeviceIdType.MESH
BF16 = jnp.bfloat16
F32 = jnp.float32
FAR_FIRST = (4, 5, 3, 6, 2, 7, 1)
N_WIRES = 176
VMEM_BYTES = 60 * 1024 * 1024


def dot(a, b):
    return jnp.dot(a, b, preferred_element_type=F32)


def dot_t(a, b):
    return lax.dot_general(a, b, (((1,), (1,)), ((), ())), preferred_element_type=F32)


def rows(start, size):
    return pl.ds(pl.multiple_of(start, size), size)


def ctx_of(x, zh, core):
    return x * 4 + zh * 2 + core


class Wires:
    def __init__(self, send_sems, recv_sems):
        self.send_sems, self.recv_sems, self.used = send_sems, recv_sems, 0

    def send(self, src, dst, to):
        at = self.used
        self.used += 1
        copy = pltpu.make_async_remote_copy(
            src_ref=src,
            dst_ref=dst,
            send_sem=self.send_sems.at[at],
            recv_sem=self.recv_sems.at[at],
            device_id=to,
            device_id_type=MESH,
        )
        copy.start()
        return copy


def wait_all(copies):
    for copy in copies:
        copy.wait()


def kernel(
    hidden_hbm,
    qd_hbm,
    ld_hbm,
    qg_hbm,
    lg_hbm,
    qup_hbm,
    ka_hbm,
    va_hbm,
    wo_hbm,
    doc_hbm,
    pos_hbm,
    freq_hbm,
    out_ref,
    hidden_ref,
    qd_ref,
    ld_ref,
    qg_ref,
    lg_ref,
    qup_ref,
    ka_ref,
    va_ref,
    wo_ref,
    doc_ref,
    pos_ref,
    freq_ref,
    gain_ref,
    lgain_ref,
    cos_ref,
    sin_ref,
    kv_out,
    kv_in,
    q_out,
    q_in,
    kv_own,
    q_own,
    kvz_out,
    kvz_in,
    qz_out,
    qz_in,
    kz_ref,
    q_ref,
    k_ref,
    qc_ref,
    s_ref,
    factor_ref,
    ho_ref,
    g_ref,
    own_ref,
    z_out,
    z_half,
    pair_out,
    z_in,
    fin_out,
    fin_ref,
    load_sems,
    send_sems,
    recv_sems,
):
    ctx = lax.axis_index("ctx")
    head = lax.axis_index("head")
    x, zh, core = ctx // 4, (ctx // 2) % 2, ctx % 2
    y, z = head // NZ, head % NZ
    ys = [lax.rem(y + d, NY) for d in range(NY)]
    zs = [lax.rem(z + d, NZ) for d in range(NZ)]
    other = 1 - zh
    far = ctx_of(x, other, core)
    to_y = [(ctx, ys[d] * NZ + z) for d in range(NY)]
    to_z = [(ctx, y * NZ + zs[d]) for d in range(NZ)]
    to_far = [(far, y * NZ + zs[d]) for d in range(NZ)]
    to_x = [(ctx_of(lax.rem(x + d, NX), zh, core), head) for d in range(NX)]
    to_core = (ctx_of(x, zh, 1 - core), head)
    wires = Wires(send_sems, recv_sems)

    loads = {}
    for i, (name, src, dst) in enumerate(
        [
            ("hidden", hidden_hbm, hidden_ref),
            ("ld", ld_hbm, ld_ref),
            ("qd", qd_hbm, qd_ref),
            ("qg", qg_hbm, qg_ref),
            ("lg", lg_hbm, lg_ref),
            ("pos", pos_hbm, pos_ref),
            ("doc", doc_hbm, doc_ref),
            ("freq", freq_hbm, freq_ref),
            ("qup", qup_hbm, qup_ref),
            ("ka", ka_hbm, ka_ref),
            ("va", va_hbm, va_ref),
            ("wo", wo_hbm, wo_ref.at[y]),
        ]
    ):
        loads[name] = pltpu.make_async_copy(src, dst, load_sems.at[i])
        loads[name].start()
    barrier = pltpu.get_barrier_semaphore()
    partners = to_y[1:] + to_z[1:] + to_far + to_x[1:] + [to_core]
    for to in partners:
        pl.semaphore_signal(barrier, inc=1, device_id=to, device_id_type=MESH)
    pl.semaphore_wait(barrier, len(partners))

    loads["hidden"].wait()
    loads["ld"].wait()
    hid = hidden_ref[...].T
    rot = dot(hid, ld_ref[:, LATENT:])
    rot = jnp.concatenate([rot, jnp.zeros_like(rot)], axis=1)
    kv_y = []
    for d in (2, 1, 3):
        kv_out[d - 1, :, 0:128] = dot(hid, ld_ref[:, rows(ys[d] * 128, 128)]).astype(BF16)
        kv_out[d - 1, :, 128:256] = rot.astype(BF16)
        kv_y.append(wires.send(kv_out.at[d - 1], kv_in.at[d - 1], to_y[d]))
    l_cols = rows(y * 128, 128)
    q_cols = rows(y * 384, 384)
    kv_own[:, 0:128] = dot(hid, ld_ref[:, l_cols])
    kv_own[:, 128:256] = rot
    loads["qd"].wait()
    for d in (2, 1, 3):
        q_out[d - 1] = dot(hid, qd_ref[:, rows(ys[d] * 384, 384)]).astype(BF16)
    q_own[...] = dot(hid, qd_ref[:, q_cols])

    def over_y(copies, own, received):
        wait_all(copies)
        total = own[...]
        for d in range(NY - 1):
            total = total + received[d].astype(F32)
        own[...] = total
        return total

    def to_all_z(total, out, received):
        for i in range(NZ):
            out[i] = total[16 * i : 16 * i + 16].astype(BF16)
        return [wires.send(out.at[zs[d]], received.at[d - 1], to_z[d]) for d in FAR_FIRST]

    here = rows(z * 16, 16)

    def over_z(copies, own, received):
        wait_all(copies)
        total = own[here, :]
        for d in range(NZ - 1):
            total = total + received[d].astype(F32)
        return total

    kv_z = to_all_z(over_y(kv_y, kv_own, kv_in), kvz_out, kvz_in)
    q_y = [wires.send(q_out.at[d - 1], q_in.at[d - 1], to_y[d]) for d in (2, 1, 3)]
    loads["pos"].wait()
    loads["freq"].wait()
    freq = jnp.broadcast_to(freq_ref[...][None, :], (128, 128)).T[: ROPE // 2]
    angles = freq * pos_ref[...].astype(F32)[None, :]
    cosine, sine = jnp.cos(angles), jnp.sin(angles)
    cos_ref[...] = jnp.concatenate([cosine, cosine, cosine, cosine], axis=0).T
    sin_ref[...] = jnp.concatenate([-sine, sine, -sine, sine], axis=0).T
    loads["qg"].wait()
    loads["lg"].wait()
    gain_ref[...] = qg_ref[...][None, :]
    lgain_ref[...] = lg_ref[...][None, :]

    mine = over_z(kv_z, kv_own, kvz_in)
    lat, rot = mine[:, :128], mine[:, 128:]
    half = ROPE // 2
    swapped = jnp.concatenate([rot[:, half:ROPE], rot[:, :half]], axis=1)
    turned = rot[:, :ROPE] * cos_ref[here, :ROPE] + swapped * sin_ref[here, :ROPE]
    kz_ref[zh, here, 128:256] = jnp.concatenate([turned, jnp.zeros_like(turned)], axis=1).astype(BF16)
    kz_ref[zh, here, 0:128] = lat.astype(BF16)
    piece = kz_ref.at[zh, here]
    kz = [wires.send(piece, piece, to_z[d]) for d in FAR_FIRST]
    kz += [wires.send(piece, piece, to_far[d]) for d in range(NZ)]
    q_z = to_all_z(over_y(q_y, q_own, q_in), qz_out, qz_in)
    loads["wo"].wait()
    weights = []

    def share_weights(i):
        size = wo_ref.shape[1] // 4
        piece = wo_ref.at[y, i * size : i * size + size, :]
        weights.extend(wires.send(piece, piece, to_y[d]) for d in (2, 1, 3))

    share_weights(0)

    def key_rows(d, i):
        return rows(ctx_of(lax.rem(x + NX - d, NX), i, core) * 128, 128)

    wait_all(kz)
    for i in range(2):
        k_ref[key_rows(0, i), l_cols] = kz_ref[i, :, 0:128]
        k_ref[key_rows(0, i), LATENT:KEY] = kz_ref[i, :, 128:256]

    def key_over_y(d, i):
        piece = k_ref.at[key_rows(d, i), l_cols]
        return [wires.send(piece, piece, to_y[e]) for e in (2, 1, 3)]

    first_y = key_over_y(0, 0)
    second_x, second_y = {}, {}
    for d in (2, 1, 3):
        second_x[d] = []
        for cols in (l_cols, pl.ds(LATENT, 128)):
            piece = k_ref.at[key_rows(0, 1), cols]
            second_x[d].append(wires.send(piece, piece, to_x[d]))
    second_y[0] = key_over_y(0, 1)
    q_low = over_z(q_z, q_own, qz_in)
    q_ref[here, q_cols] = (q_low * gain_ref[:, q_cols]).astype(BF16)
    piece = q_ref.at[here, q_cols]
    qz = [wires.send(piece, piece, to_z[d]) for d in FAR_FIRST]
    wait_all(first_y)
    first_x = {}
    for d in (2, 1, 3):
        piece = k_ref.at[key_rows(0, 0), :]
        first_x[d] = [wires.send(piece, piece, to_x[d])]
    for d in (1, 3, 2):
        wait_all(second_x[d])
        second_y[d] = key_over_y(d, 1)
    wait_all(qz)
    piece = q_ref.at[:, q_cols]
    q_all = [wires.send(piece, piece, to_y[d]) for d in (2, 1, 3)]

    key_core = {}

    def key_to_core(d):
        if d:
            wait_all(first_x[d])
        wait_all(second_y[d])
        key_core[d] = []
        for i in range(2):
            piece = k_ref.at[key_rows(d, i), :]
            key_core[d].append(wires.send(piece, piece, to_core))

    for name in ("qup", "ka", "va", "doc"):
        loads[name].wait()
    key_to_core(0)
    wait_all(q_all)
    share_weights(1)
    plain = q_ref[...].astype(F32) / gain_ref[...]
    mean = jnp.sum(plain * plain, axis=1, keepdims=True) / QRANK
    full = dot(q_ref[...], qup_ref[...]) * lax.rsqrt(mean + 1e-06)
    lgain = lgain_ref[...]
    cosine, sine = cos_ref[:, :ROPE], sin_ref[:, :ROPE]
    for h in range(4):
        at = h * (NOPE + ROPE)
        nope = full[:, at : at + NOPE].astype(BF16)
        raw = full[:, at + NOPE : at + NOPE + ROPE]
        swapped = jnp.concatenate([raw[:, half:], raw[:, :half]], axis=1)
        turned = raw * cosine + swapped * sine
        low = dot_t(nope, ka_ref[:, h * NOPE : (h + 1) * NOPE])
        mine = slice(h * 128, h * 128 + 128)
        qc_ref[mine, :LATENT] = (low * lgain).astype(BF16)
        qc_ref[mine, LATENT:] = jnp.concatenate([turned, jnp.zeros_like(turned)], axis=1).astype(BF16)

    doc = jnp.broadcast_to(doc_ref[...].astype(F32)[None, :], (128, 128)).T[:, 0:1].astype(jnp.int32)
    query_index = ctx * 128 + lax.broadcasted_iota(jnp.int32, (128, 512), 0)
    key_lane = lax.broadcasted_iota(jnp.int32, (128, 512), 1)
    top = [None] * 4

    def scores(d):
        wait_all(key_core[d])
        at = rows(lax.rem(x + NX - d, NX) * 512, 512)
        key_index = key_lane + lax.rem(x + NX - d, NX) * 512
        bias = jnp.where((key_index <= query_index) & (key_index >= doc), 0.0, -1e30)
        keys = k_ref[at, :LATENT]
        wide = keys.astype(F32)
        mean = dot_t(jnp.ones((8, LATENT), BF16), (wide * wide).astype(BF16)) / LATENT
        factor = lax.rsqrt(mean + 1e-06)
        factor_ref[:, at] = factor
        factor = factor[0:1] * SCALE
        block = dot_t(qc_ref[:, :LATENT], keys)
        turn = dot_t(qc_ref[:, LATENT:], k_ref[at, LATENT:])
        for h in range(4):
            mine = slice(h * 128, h * 128 + 128)
            values = block[mine] * factor + (turn[mine] * SCALE + bias)
            s_ref[mine, at] = values
            most = jnp.max(values, axis=1, keepdims=True)
            top[h] = most if top[h] is None else jnp.maximum(top[h], most)

    key_to_core(1)
    scores(0)
    key_to_core(3)
    scores(1)
    key_to_core(2)
    scores(3)
    scores(2)

    here_zc, far_zc = zh * 2 + core, other * 2 + core
    cols = rows(y * 256, 256)

    def mix(pair, between):
        mine = slice(pair * 256, pair * 256 + 256)
        most = jnp.concatenate([top[2 * pair], top[2 * pair + 1]], axis=0)
        weighted = jnp.zeros((256, LATENT), F32)
        total = jnp.zeros((256, 1), F32)
        for j in range(4):
            span = slice(512 * j, 512 * j + 512)
            expo = jnp.exp(s_ref[mine, span] - most)
            total = total + jnp.sum(expo, axis=1, keepdims=True)
            expo = expo * factor_ref[0:1, span]
            weighted = weighted + dot(expo.astype(BF16), k_ref[span, :LATENT])
        between()
        mixed = (weighted * lgain / total).astype(BF16)
        for i in range(2):
            at = (2 * pair + i) * VDIM
            result = dot(mixed[128 * i : 128 * i + 128], va_ref[:, at : at + VDIM]).astype(BF16)
            for part in range(4):
                for side in range(2):
                    first = 64 * side + 16 * part
                    ho_ref[pair, part, side, :, 128 * i : 128 * i + 128] = result[first : first + 16]
        g_ref[pair, here_zc, :, x, :, cols] = ho_ref[pair, y]
        spot = g_ref.at[pair, here_zc, :, x, :, cols]
        return [wires.send(ho_ref.at[pair, ys[d]], spot, to_y[d]) for d in (2, 1, 3)]

    def block(pair, zc, d):
        return g_ref.at[pair, zc, :, lax.rem(x + NX - d, NX)]

    def spread(pair, zc, over_x):
        piece = block(pair, zc, 0)
        for d in (2, 1, 3):
            over_x[pair, zc is far_zc, d] = wires.send(piece, piece, to_x[d])
        return wires.send(piece, piece, to_core)

    over_x, over_core, over_far = {}, [], {}

    def launch(pair, copies):
        wait_all(copies)
        piece = block(pair, here_zc, 0)
        over_far[pair] = wires.send(piece, piece, to_far[0])
        over_core.append(spread(pair, here_zc, over_x))

    handed = mix(0, lambda: None)
    second = mix(1, lambda: launch(0, handed))
    launch(1, second)
    share_weights(2)
    share_weights(3)
    for pair in range(2):
        over_far[pair].wait()
        over_core.append(spread(pair, far_zc, over_x))
    for pair in range(2):
        for zc in (here_zc, far_zc):
            for d in (1, 3, 2):
                over_x[pair, zc is far_zc, d].wait()
                piece = block(pair, zc, d)
                over_core.append(wires.send(piece, piece, to_core))
    wait_all(over_core)
    wait_all(weights)

    pair_at, odd = z // 2, z % 2
    near = (ctx, y * NZ + pair_at * 2 + 1 - odd)
    halves, sums = {}, {}
    for k in (2, 1, 3, 0):
        zc = lax.rem(pair_at + k, 4)
        total = jnp.zeros((128, out_ref.shape[1]), F32)
        for pair in range(2):
            tokens = g_ref[pair, zc].reshape(128, 1024)
            for i in range(NY):
                total = total + dot_t(
                    tokens[:, 256 * i : 256 * i + 256], wo_ref[i, :, 256 * pair : 256 * pair + 256]
                )
        for side in range(2):
            part = total[64 * side : 64 * side + 64]
            part = jnp.concatenate([part[:32], part[32:]], axis=1)
            own_ref[k, side] = part
            z_out[k, side] = part.astype(BF16)
        halves[k] = wires.send(z_out.at[k, 1 - odd], z_half.at[k], near)
    for k in (2, 1, 3):
        halves[k].wait()
        pair_out[k] = (own_ref[k, odd] + z_half[k].astype(F32)).astype(BF16)
        to = (ctx, y * NZ + lax.rem(pair_at + k, 4) * 2 + odd)
        sums[k] = wires.send(pair_out.at[k], z_in.at[k], to)
    halves[0].wait()
    total = own_ref[0, odd] + z_half[0].astype(F32)
    for k in (1, 3, 2):
        sums[k].wait()
        total = total + z_in[k].astype(F32)
    width = out_ref.shape[1]
    result = jnp.concatenate([total[:, :width], total[:, width:]], axis=0).astype(BF16)
    for i in range(NX):
        fin_out[i] = result[16 * i : 16 * i + 16]
    fin_ref[y] = fin_out[y]
    wait_all([wires.send(fin_out.at[ys[d]], fin_ref.at[y], to_y[d]) for d in (2, 1, 3)])
    for i in range(NY):
        out_ref[16 * i : 16 * i + 16, :] = fin_ref[i]
    assert wires.used <= N_WIRES


def body(
    hidden,
    query_down,
    latent_down,
    query_gain,
    latent_gain,
    query_up,
    key_absorb,
    value_absorb,
    out_proj,
    doc_start,
    positions,
):
    half = ROPE // 2
    freqs = np.zeros((128,), np.float32)
    freqs[:half] = 10000.0 ** (-2.0 * np.arange(half) / ROPE)
    width = out_proj.shape[1]
    hidden, out_proj = hidden.T, out_proj.T
    vmem = pltpu.VMEM
    operands = (
        hidden,
        query_down,
        latent_down,
        query_gain,
        latent_gain,
        query_up,
        key_absorb,
        value_absorb,
        out_proj,
        doc_start,
        positions,
        jnp.asarray(freqs),
    )
    scratch = [vmem(a.shape, a.dtype) for a in operands]
    scratch[8] = vmem((NY,) + out_proj.shape, BF16)
    scratch += [
        vmem((1, QRANK), F32),
        vmem((1, LATENT), F32),
        vmem((128, 128), F32),
        vmem((128, 128), F32),
        vmem((3, 128, 256), BF16),
        vmem((3, 128, 256), BF16),
        vmem((3, 128, 384), BF16),
        vmem((3, 128, 384), BF16),
        vmem((128, 256), F32),
        vmem((128, 384), F32),
        vmem((8, 16, 256), BF16),
        vmem((7, 16, 256), BF16),
        vmem((8, 16, 384), BF16),
        vmem((7, 16, 384), BF16),
        vmem((2, 128, 256), BF16),
        vmem((128, QRANK), BF16),
        vmem((2048, KEY), BF16),
        vmem((512, KEY), BF16),
        vmem((512, 2048), F32),
        vmem((8, 2048), F32),
        vmem((2, 4, 2, 16, 256), BF16),
        vmem((2, 4, 2, 4, 16, 1024), BF16),
        vmem((4, 2, 32, 2 * width), F32),
        vmem((4, 2, 32, 2 * width), BF16),
        vmem((4, 32, 2 * width), BF16),
        vmem((4, 32, 2 * width), BF16),
        vmem((4, 32, 2 * width), BF16),
        vmem((4, 16, width), BF16),
        vmem((4, 16, width), BF16),
        pltpu.SemaphoreType.DMA((len(operands),)),
        pltpu.SemaphoreType.DMA((N_WIRES,)),
        pltpu.SemaphoreType.DMA((N_WIRES,)),
    ]
    return pl.pallas_call(
        kernel,
        out_shape=jax.ShapeDtypeStruct((64, width), BF16),
        in_specs=[pl.BlockSpec(memory_space=pl.ANY)] * len(operands),
        out_specs=pl.BlockSpec(memory_space=pltpu.VMEM),
        scratch_shapes=scratch,
        compiler_params=pltpu.CompilerParams(
            collective_id=0, has_side_effects=True, vmem_limit_bytes=VMEM_BYTES
        ),
        name="latent_attention",
    )(*operands)


def solution(mesh):
    in_specs = (
        P("ctx", "head"),
        P("head", None),
        P("head", None),
        P(),
        P(),
        P(None, "head"),
        P(None, "head"),
        P(None, "head"),
        P("head", "ctx"),
        P("ctx"),
        P("ctx"),
    )
    out_specs = P("head", "ctx")
    return jax.shard_map(body, mesh=mesh, in_specs=in_specs, out_specs=out_specs, check_vma=False)
```

```python
import jax
import jax.numpy as jnp
import numpy as np
from jax import lax
from jax.experimental import pallas as pl
from jax.experimental.pallas import tpu as pltpu
from jax.sharding import PartitionSpec as P

LATENT = 512
ROPE = 64
NOPE = 128
VDIM = 128
QRANK = 1536
NX, NY, NZ = 4, 4, 8
KEY = LATENT + 2 * ROPE
SCALE = (NOPE + ROPE) ** (-0.5)
MESH = pl.DeviceIdType.MESH
BF16 = jnp.bfloat16
F32 = jnp.float32
FAR_FIRST = (4, 5, 3, 6, 2, 7, 1)
N_WIRES = 224
VMEM_BYTES = 60 * 1024 * 1024


def dot(a, b):
    return jnp.dot(a, b, preferred_element_type=F32)


def dot_t(a, b):
    return lax.dot_general(a, b, (((1,), (1,)), ((), ())), preferred_element_type=F32)


def rows(start, size):
    return pl.ds(pl.multiple_of(start, size), size)


def ctx_of(x, zh, core):
    return x * 4 + zh * 2 + core


class Wires:
    def __init__(self, send_sems, recv_sems):
        self.send_sems, self.recv_sems, self.used = send_sems, recv_sems, 0

    def send(self, src, dst, to):
        at = self.used
        self.used += 1
        copy = pltpu.make_async_remote_copy(
            src_ref=src,
            dst_ref=dst,
            send_sem=self.send_sems.at[at],
            recv_sem=self.recv_sems.at[at],
            device_id=to,
            device_id_type=MESH,
        )
        copy.start()
        return copy


def wait_all(copies):
    for copy in copies:
        copy.wait()


def kernel(
    hidden_hbm,
    qd_hbm,
    ld_hbm,
    qg_hbm,
    lg_hbm,
    qup_hbm,
    ka_hbm,
    va_hbm,
    wo_hbm,
    doc_hbm,
    pos_hbm,
    freq_hbm,
    out_ref,
    hidden_ref,
    qd_ref,
    ld_ref,
    qg_ref,
    lg_ref,
    qup_ref,
    ka_ref,
    va_ref,
    wo_ref,
    doc_ref,
    pos_ref,
    freq_ref,
    gain_ref,
    lgain_ref,
    cos_ref,
    sin_ref,
    kv_out,
    kv_in,
    q_out,
    q_in,
    kv_own,
    q_own,
    kvz_out,
    kvz_in,
    qz_out,
    qz_in,
    kz_ref,
    q_ref,
    k_ref,
    qc_ref,
    s_ref,
    factor_ref,
    ho_ref,
    g_ref,
    own_ref,
    z_out,
    z_half,
    pair_out,
    z_in,
    fin_out,
    fin_ref,
    load_sems,
    send_sems,
    recv_sems,
):
    ctx = lax.axis_index("ctx")
    head = lax.axis_index("head")
    x, zh, core = ctx // 4, (ctx // 2) % 2, ctx % 2
    y, z = head // NZ, head % NZ
    ys = [lax.rem(y + d, NY) for d in range(NY)]
    zs = [lax.rem(z + d, NZ) for d in range(NZ)]
    other = 1 - zh
    far = ctx_of(x, other, core)
    to_y = [(ctx, ys[d] * NZ + z) for d in range(NY)]
    to_z = [(ctx, y * NZ + zs[d]) for d in range(NZ)]
    to_far = [(far, y * NZ + zs[d]) for d in range(NZ)]
    to_x = [(ctx_of(lax.rem(x + d, NX), zh, core), head) for d in range(NX)]
    to_core = (ctx_of(x, zh, 1 - core), head)
    wires = Wires(send_sems, recv_sems)

    loads = {}
    for i, (name, src, dst) in enumerate(
        [
            ("hidden", hidden_hbm, hidden_ref),
            ("ld", ld_hbm, ld_ref),
            ("qd", qd_hbm, qd_ref),
            ("qg", qg_hbm, qg_ref),
            ("lg", lg_hbm, lg_ref),
            ("pos", pos_hbm, pos_ref),
            ("doc", doc_hbm, doc_ref),
            ("freq", freq_hbm, freq_ref),
            ("qup", qup_hbm, qup_ref),
            ("ka", ka_hbm, ka_ref),
            ("va", va_hbm, va_ref),
            ("wo", wo_hbm, wo_ref.at[y]),
        ]
    ):
        loads[name] = pltpu.make_async_copy(src, dst, load_sems.at[i])
        loads[name].start()
    barrier = pltpu.get_barrier_semaphore()
    partners = to_y[1:] + to_z[1:] + to_far + to_x[1:] + [to_core]
    for to in partners:
        pl.semaphore_signal(barrier, inc=1, device_id=to, device_id_type=MESH)
    pl.semaphore_wait(barrier, len(partners))

    loads["hidden"].wait()
    loads["ld"].wait()
    hid = hidden_ref[...].T
    rot = dot(hid, ld_ref[:, LATENT:])
    rot = jnp.concatenate([rot, jnp.zeros_like(rot)], axis=1)
    kv_y = []
    for d in (2, 1, 3):
        kv_out[d - 1, :, 0:128] = dot(hid, ld_ref[:, rows(ys[d] * 128, 128)]).astype(BF16)
        kv_out[d - 1, :, 128:256] = rot.astype(BF16)
        kv_y.append(wires.send(kv_out.at[d - 1], kv_in.at[d - 1], to_y[d]))
    l_cols = rows(y * 128, 128)
    q_cols = rows(y * 384, 384)
    kv_own[:, 0:128] = dot(hid, ld_ref[:, l_cols])
    kv_own[:, 128:256] = rot
    loads["qd"].wait()
    for d in (2, 1, 3):
        q_out[d - 1] = dot(hid, qd_ref[:, rows(ys[d] * 384, 384)]).astype(BF16)
    q_own[...] = dot(hid, qd_ref[:, q_cols])

    def over_y(copies, own, received):
        wait_all(copies)
        total = own[...]
        for d in range(NY - 1):
            total = total + received[d].astype(F32)
        own[...] = total
        return total

    def to_all_z(total, out, received):
        for i in range(NZ):
            out[i] = total[16 * i : 16 * i + 16].astype(BF16)
        return [wires.send(out.at[zs[d]], received.at[d - 1], to_z[d]) for d in FAR_FIRST]

    here = rows(z * 16, 16)

    def over_z(copies, own, received):
        wait_all(copies)
        total = own[here, :]
        for d in range(NZ - 1):
            total = total + received[d].astype(F32)
        return total

    kv_z = to_all_z(over_y(kv_y, kv_own, kv_in), kvz_out, kvz_in)
    q_y = [wires.send(q_out.at[d - 1], q_in.at[d - 1], to_y[d]) for d in (2, 1, 3)]
    loads["pos"].wait()
    loads["freq"].wait()
    freq = jnp.broadcast_to(freq_ref[...][None, :], (128, 128)).T[: ROPE // 2]
    angles = freq * pos_ref[...].astype(F32)[None, :]
    cosine, sine = jnp.cos(angles), jnp.sin(angles)
    cos_ref[...] = jnp.concatenate([cosine, cosine, cosine, cosine], axis=0).T
    sin_ref[...] = jnp.concatenate([-sine, sine, -sine, sine], axis=0).T
    loads["qg"].wait()
    loads["lg"].wait()
    gain_ref[...] = qg_ref[...][None, :]
    lgain_ref[...] = lg_ref[...][None, :]

    mine = over_z(kv_z, kv_own, kvz_in)
    lat, rot = mine[:, :128], mine[:, 128:]
    half = ROPE // 2
    swapped = jnp.concatenate([rot[:, half:ROPE], rot[:, :half]], axis=1)
    turned = rot[:, :ROPE] * cos_ref[here, :ROPE] + swapped * sin_ref[here, :ROPE]
    kz_ref[zh, here, 128:256] = jnp.concatenate([turned, jnp.zeros_like(turned)], axis=1).astype(BF16)
    kz_ref[zh, here, 0:128] = lat.astype(BF16)
    piece = kz_ref.at[zh, here]
    kz = [wires.send(piece, piece, to_z[d]) for d in FAR_FIRST]
    kz += [wires.send(piece, piece, to_far[d]) for d in range(NZ)]
    q_z = to_all_z(over_y(q_y, q_own, q_in), qz_out, qz_in)
    loads["wo"].wait()
    weights = []

    def share_weights(i):
        size = wo_ref.shape[1] // 4
        piece = wo_ref.at[y, i * size : i * size + size, :]
        weights.extend(wires.send(piece, piece, to_y[d]) for d in (2, 1, 3))

    share_weights(0)

    def key_rows(d, i):
        return rows(ctx_of(lax.rem(x + NX - d, NX), i, core) * 128, 128)

    wait_all(kz)
    for i in range(2):
        k_ref[key_rows(0, i), l_cols] = kz_ref[i, :, 0:128]
        k_ref[key_rows(0, i), LATENT:KEY] = kz_ref[i, :, 128:256]

    def key_over_y(d, i):
        piece = k_ref.at[key_rows(d, i), l_cols]
        return [wires.send(piece, piece, to_y[e]) for e in (2, 1, 3)]

    first_y = key_over_y(0, 0)
    second_x, second_y = {}, {}
    for d in (2, 1, 3):
        second_x[d] = []
        for cols in (l_cols, pl.ds(LATENT, 128)):
            piece = k_ref.at[key_rows(0, 1), cols]
            second_x[d].append(wires.send(piece, piece, to_x[d]))
    second_y[0] = key_over_y(0, 1)
    q_low = over_z(q_z, q_own, qz_in)
    q_ref[here, q_cols] = (q_low * gain_ref[:, q_cols]).astype(BF16)
    piece = q_ref.at[here, q_cols]
    qz = [wires.send(piece, piece, to_z[d]) for d in FAR_FIRST]
    wait_all(first_y)
    first_x = {}
    for d in (2, 1, 3):
        piece = k_ref.at[key_rows(0, 0), :]
        first_x[d] = [wires.send(piece, piece, to_x[d])]
    for d in (1, 3, 2):
        wait_all(second_x[d])
        second_y[d] = key_over_y(d, 1)
    wait_all(qz)
    piece = q_ref.at[:, q_cols]
    q_all = [wires.send(piece, piece, to_y[d]) for d in (2, 1, 3)]

    key_core = {}

    def key_to_core(d):
        if d:
            wait_all(first_x[d])
        wait_all(second_y[d])
        key_core[d] = []
        for i in range(2):
            piece = k_ref.at[key_rows(d, i), :]
            key_core[d].append(wires.send(piece, piece, to_core))

    for name in ("qup", "ka", "va", "doc"):
        loads[name].wait()
    key_to_core(0)
    wait_all(q_all)
    share_weights(1)
    plain = q_ref[...].astype(F32) / gain_ref[...]
    mean = jnp.sum(plain * plain, axis=1, keepdims=True) / QRANK
    full = dot(q_ref[...], qup_ref[...]) * lax.rsqrt(mean + 1e-06)
    lgain = lgain_ref[...]
    cosine, sine = cos_ref[:, :ROPE], sin_ref[:, :ROPE]
    for h in range(4):
        at = h * (NOPE + ROPE)
        nope = full[:, at : at + NOPE].astype(BF16)
        raw = full[:, at + NOPE : at + NOPE + ROPE]
        swapped = jnp.concatenate([raw[:, half:], raw[:, :half]], axis=1)
        turned = raw * cosine + swapped * sine
        low = dot_t(nope, ka_ref[:, h * NOPE : (h + 1) * NOPE])
        mine = slice(h * 128, h * 128 + 128)
        qc_ref[mine, :LATENT] = (low * lgain).astype(BF16)
        qc_ref[mine, LATENT:] = jnp.concatenate([turned, jnp.zeros_like(turned)], axis=1).astype(BF16)

    doc = jnp.broadcast_to(doc_ref[...].astype(F32)[None, :], (128, 128)).T[:, 0:1].astype(jnp.int32)
    query_index = ctx * 128 + lax.broadcasted_iota(jnp.int32, (128, 512), 0)
    key_lane = lax.broadcasted_iota(jnp.int32, (128, 512), 1)
    top = [None] * 4

    def scores(d):
        wait_all(key_core[d])
        at = rows(lax.rem(x + NX - d, NX) * 512, 512)
        key_index = key_lane + lax.rem(x + NX - d, NX) * 512
        bias = jnp.where((key_index <= query_index) & (key_index >= doc), 0.0, -1e30)
        keys = k_ref[at, :LATENT]
        wide = keys.astype(F32)
        mean = dot_t(jnp.ones((8, LATENT), BF16), (wide * wide).astype(BF16)) / LATENT
        factor = lax.rsqrt(mean + 1e-06)
        factor_ref[:, at] = factor
        factor = factor[0:1] * SCALE
        block = dot_t(qc_ref[:, :LATENT], keys)
        turn = dot_t(qc_ref[:, LATENT:], k_ref[at, LATENT:])
        for h in range(4):
            mine = slice(h * 128, h * 128 + 128)
            values = block[mine] * factor + (turn[mine] * SCALE + bias)
            s_ref[mine, at] = values
            most = jnp.max(values, axis=1, keepdims=True)
            top[h] = most if top[h] is None else jnp.maximum(top[h], most)

    key_to_core(1)
    scores(0)
    key_to_core(3)
    scores(1)
    key_to_core(2)
    scores(3)
    scores(2)

    cols = rows(y * 256, 256)

    def mix(pair):
        mine = slice(pair * 256, pair * 256 + 256)
        most = jnp.concatenate([top[2 * pair], top[2 * pair + 1]], axis=0)
        weighted = jnp.zeros((256, LATENT), F32)
        total = jnp.zeros((256, 1), F32)
        for j in range(4):
            span = slice(512 * j, 512 * j + 512)
            expo = jnp.exp(s_ref[mine, span] - most)
            total = total + jnp.sum(expo, axis=1, keepdims=True)
            expo = expo * factor_ref[0:1, span]
            weighted = weighted + dot(expo.astype(BF16), k_ref[span, :LATENT])
        mixed = (weighted * lgain / total).astype(BF16)
        for i in range(2):
            at = (2 * pair + i) * VDIM
            result = dot(mixed[128 * i : 128 * i + 128], va_ref[:, at : at + VDIM]).astype(BF16)
            for part in range(4):
                for side in range(2):
                    first = 64 * side + 16 * part
                    ho_ref[pair, part, side, :, 128 * i : 128 * i + 128] = result[first : first + 16]
        g_ref[pair, core, :, x, :, cols] = ho_ref[pair, y]
        spot = g_ref.at[pair, core, :, x, :, cols]
        return [wires.send(ho_ref.at[pair, ys[d]], spot, to_y[d]) for d in (2, 1, 3)]

    def block(pair, side, d):
        return g_ref.at[pair, core, side, lax.rem(x + NX - d, NX)]

    def far_block(pair, side, d):
        return g_ref.at[pair, 2 + core, side, lax.rem(x + NX - d, NX)]

    over_far, over_x, own_core, far_core = {}, {}, [], []

    def launch(pair, copies):
        wait_all(copies)
        for side in range(2):
            over_far[pair, side] = wires.send(
                block(pair, side, 0), far_block(pair, side, 0), to_far[0]
            )
        piece = block(pair, slice(None), 0)
        for d in (2, 1, 3):
            over_x[pair, d] = wires.send(piece, piece, to_x[d])
        own_core.append(wires.send(piece, piece, to_core))

    handed = [mix(0), mix(1)]
    launch(0, handed[0])
    launch(1, handed[1])
    share_weights(2)
    share_weights(3)

    def spread(pair):
        for side in range(2):
            over_far[pair, side].wait()
            piece = far_block(pair, side, 0)
            for d in (2, 1, 3):
                over_x[pair, side, d] = wires.send(piece, piece, to_x[d])
            far_core.append(wires.send(piece, piece, to_core))

    spread(0)
    for pair in range(2):
        for d in (1, 3, 2):
            over_x[pair, d].wait()
            piece = block(pair, slice(None), d)
            own_core.append(wires.send(piece, piece, to_core))
    spread(1)

    pair_at, odd = z // 2, z % 2
    near = (ctx, y * NZ + pair_at * 2 + 1 - odd)
    halves = {}
    last = wires.used + 8
    wires.used += 16

    def product(j):
        total = jnp.zeros((128, out_ref.shape[1]), F32)
        for pair in range(2):
            tokens = g_ref[pair, j].reshape(128, 1024)
            for i in range(NY):
                total = total + dot_t(
                    tokens[:, 256 * i : 256 * i + 256], wo_ref[i, :, 256 * pair : 256 * pair + 256]
                )
        for side in range(2):
            part = total[64 * side : 64 * side + 64]
            part = jnp.concatenate([part[:32], part[32:]], axis=1)
            own_ref[j, side] = part
            z_out[j, side] = part.astype(BF16)
        halves[j] = wires.send(z_out.at[j, 1 - odd], z_half.at[j], near)

    def pair_of(j):
        return 2 * (zh, other)[j // 2] + j % 2

    def pair_copy(j):
        away = lax.rem(pair_of(j) - pair_at + 4, 4)
        copy = pltpu.make_async_remote_copy(
            src_ref=pair_out.at[j],
            dst_ref=z_in.at[away],
            send_sem=send_sems.at[last + j],
            recv_sem=recv_sems.at[last + away],
            device_id=(ctx, y * NZ + pair_of(j) * 2 + odd),
            device_id_type=MESH,
        )
        return away, copy

    def pass_on(j):
        halves[j].wait()
        total = own_ref[j, odd] + z_half[j].astype(F32)
        own_ref[j, odd] = total
        pair_out[j] = total.astype(BF16)
        away, copy = pair_copy(j)

        @pl.when(away != 0)
        def _():
            copy.start()

    def forward(pair):
        for side in range(2):
            for d in (1, 3, 2):
                over_x[pair, side, d].wait()
                piece = far_block(pair, side, d)
                far_core.append(wires.send(piece, piece, to_core))

    wait_all(own_core)
    wait_all(weights)
    product(0)
    product(1)
    forward(0)
    pass_on(0)
    pass_on(1)
    forward(1)
    wait_all(far_core)
    product(2)
    product(3)
    pass_on(2)
    pass_on(3)
    half_at = pair_at // 2
    total = own_ref[pair_at % 2 + 2 * (half_at + zh - 2 * half_at * zh), odd]
    for away in (1, 3, 2):
        pltpu.make_async_remote_copy(
            src_ref=pair_out.at[0],
            dst_ref=z_in.at[away],
            send_sem=send_sems.at[last],
            recv_sem=recv_sems.at[last + away],
            device_id=near,
            device_id_type=MESH,
        ).wait_recv()
        total = total + z_in[away].astype(F32)
    for j in range(4):
        away, copy = pair_copy(j)

        @pl.when(away != 0)
        def _(copy=copy):
            copy.wait_send()
    width = out_ref.shape[1]
    result = jnp.concatenate([total[:, :width], total[:, width:]], axis=0).astype(BF16)
    for i in range(NX):
        fin_out[i] = result[16 * i : 16 * i + 16]
    fin_ref[y] = fin_out[y]
    wait_all([wires.send(fin_out.at[ys[d]], fin_ref.at[y], to_y[d]) for d in (2, 1, 3)])
    for i in range(NY):
        out_ref[16 * i : 16 * i + 16, :] = fin_ref[i]
    assert wires.used <= N_WIRES


def body(
    hidden,
    query_down,
    latent_down,
    query_gain,
    latent_gain,
    query_up,
    key_absorb,
    value_absorb,
    out_proj,
    doc_start,
    positions,
):
    half = ROPE // 2
    freqs = np.zeros((128,), np.float32)
    freqs[:half] = 10000.0 ** (-2.0 * np.arange(half) / ROPE)
    width = out_proj.shape[1]
    hidden, out_proj = hidden.T, out_proj.T
    vmem = pltpu.VMEM
    operands = (
        hidden,
        query_down,
        latent_down,
        query_gain,
        latent_gain,
        query_up,
        key_absorb,
        value_absorb,
        out_proj,
        doc_start,
        positions,
        jnp.asarray(freqs),
    )
    scratch = [vmem(a.shape, a.dtype) for a in operands]
    scratch[8] = vmem((NY,) + out_proj.shape, BF16)
    scratch += [
        vmem((1, QRANK), F32),
        vmem((1, LATENT), F32),
        vmem((128, 128), F32),
        vmem((128, 128), F32),
        vmem((3, 128, 256), BF16),
        vmem((3, 128, 256), BF16),
        vmem((3, 128, 384), BF16),
        vmem((3, 128, 384), BF16),
        vmem((128, 256), F32),
        vmem((128, 384), F32),
        vmem((8, 16, 256), BF16),
        vmem((7, 16, 256), BF16),
        vmem((8, 16, 384), BF16),
        vmem((7, 16, 384), BF16),
        vmem((2, 128, 256), BF16),
        vmem((128, QRANK), BF16),
        vmem((2048, KEY), BF16),
        vmem((512, KEY), BF16),
        vmem((512, 2048), F32),
        vmem((8, 2048), F32),
        vmem((2, 4, 2, 16, 256), BF16),
        vmem((2, 4, 2, 4, 16, 1024), BF16),
        vmem((4, 2, 32, 2 * width), F32),
        vmem((4, 2, 32, 2 * width), BF16),
        vmem((4, 32, 2 * width), BF16),
        vmem((4, 32, 2 * width), BF16),
        vmem((4, 32, 2 * width), BF16),
        vmem((4, 16, width), BF16),
        vmem((4, 16, width), BF16),
        pltpu.SemaphoreType.DMA((len(operands),)),
        pltpu.SemaphoreType.DMA((N_WIRES,)),
        pltpu.SemaphoreType.DMA((N_WIRES,)),
    ]
    return pl.pallas_call(
        kernel,
        out_shape=jax.ShapeDtypeStruct((64, width), BF16),
        in_specs=[pl.BlockSpec(memory_space=pl.ANY)] * len(operands),
        out_specs=pl.BlockSpec(memory_space=pltpu.VMEM),
        scratch_shapes=scratch,
        compiler_params=pltpu.CompilerParams(
            collective_id=0, has_side_effects=True, vmem_limit_bytes=VMEM_BYTES
        ),
        name="latent_attention",
    )(*operands)


def solution(mesh):
    in_specs = (
        P("ctx", "head"),
        P("head", None),
        P("head", None),
        P(),
        P(),
        P(None, "head"),
        P(None, "head"),
        P(None, "head"),
        P("head", "ctx"),
        P("ctx"),
        P("ctx"),
    )
    out_specs = P("head", "ctx")
    return jax.shard_map(body, mesh=mesh, in_specs=in_specs, out_specs=out_specs, check_vma=False)
```

```python
import jax
import jax.numpy as jnp
import numpy as np
from jax import lax
from jax.experimental import pallas as pl
from jax.experimental.pallas import tpu as pltpu
from jax.sharding import PartitionSpec as P

LATENT = 512
ROPE = 64
NOPE = 128
VDIM = 128
QRANK = 1536
NX, NY, NZ = 4, 4, 8
KEY = LATENT + 2 * ROPE
SCALE = (NOPE + ROPE) ** (-0.5)
MESH = pl.DeviceIdType.MESH
BF16 = jnp.bfloat16
F32 = jnp.float32
FAR_FIRST = (4, 5, 3, 6, 2, 7, 1)
N_WIRES = 224
VMEM_BYTES = 60 * 1024 * 1024


def dot(a, b):
    return jnp.dot(a, b, preferred_element_type=F32)


def dot_t(a, b):
    return lax.dot_general(a, b, (((1,), (1,)), ((), ())), preferred_element_type=F32)


def rows(start, size):
    return pl.ds(pl.multiple_of(start, size), size)


def ctx_of(x, zh, core):
    return x * 4 + zh * 2 + core


class Wires:
    def __init__(self, send_sems, recv_sems):
        self.send_sems, self.recv_sems, self.used = send_sems, recv_sems, 0

    def send(self, src, dst, to):
        at = self.used
        self.used += 1
        copy = pltpu.make_async_remote_copy(
            src_ref=src,
            dst_ref=dst,
            send_sem=self.send_sems.at[at],
            recv_sem=self.recv_sems.at[at],
            device_id=to,
            device_id_type=MESH,
        )
        copy.start()
        return copy


def wait_all(copies):
    for copy in copies:
        copy.wait()


def kernel(
    hidden_hbm,
    qd_hbm,
    ld_hbm,
    qg_hbm,
    lg_hbm,
    qup_hbm,
    ka_hbm,
    va_hbm,
    wo_hbm,
    doc_hbm,
    pos_hbm,
    freq_hbm,
    out_ref,
    hidden_ref,
    qd_ref,
    ld_ref,
    qg_ref,
    lg_ref,
    qup_ref,
    ka_ref,
    va_ref,
    wo_ref,
    doc_ref,
    pos_ref,
    freq_ref,
    gain_ref,
    lgain_ref,
    cos_ref,
    sin_ref,
    kv_out,
    kv_in,
    q_out,
    q_in,
    kv_own,
    q_own,
    kvz_out,
    kvz_in,
    qz_out,
    qz_in,
    kz_ref,
    q_ref,
    k_ref,
    qc_ref,
    s_ref,
    factor_ref,
    ho_ref,
    g_ref,
    own_ref,
    z_out,
    z_half,
    pair_out,
    z_in,
    fin_out,
    fin_ref,
    load_sems,
    send_sems,
    recv_sems,
):
    ctx = lax.axis_index("ctx")
    head = lax.axis_index("head")
    x, zh, core = ctx // 4, (ctx // 2) % 2, ctx % 2
    y, z = head // NZ, head % NZ
    ys = [lax.rem(y + d, NY) for d in range(NY)]
    zs = [lax.rem(z + d, NZ) for d in range(NZ)]
    other = 1 - zh
    far = ctx_of(x, other, core)
    to_y = [(ctx, ys[d] * NZ + z) for d in range(NY)]
    to_z = [(ctx, y * NZ + zs[d]) for d in range(NZ)]
    to_far = [(far, y * NZ + zs[d]) for d in range(NZ)]
    to_x = [(ctx_of(lax.rem(x + d, NX), zh, core), head) for d in range(NX)]
    to_core = (ctx_of(x, zh, 1 - core), head)
    wires = Wires(send_sems, recv_sems)

    loads = {}
    for i, (name, src, dst) in enumerate(
        [
            ("hidden", hidden_hbm, hidden_ref),
            ("ld", ld_hbm, ld_ref),
            ("qd", qd_hbm, qd_ref),
            ("qg", qg_hbm, qg_ref),
            ("lg", lg_hbm, lg_ref),
            ("pos", pos_hbm, pos_ref),
            ("doc", doc_hbm, doc_ref),
            ("freq", freq_hbm, freq_ref),
            ("qup", qup_hbm, qup_ref),
            ("ka", ka_hbm, ka_ref),
            ("va", va_hbm, va_ref),
            ("wo", wo_hbm, wo_ref.at[y]),
        ]
    ):
        loads[name] = pltpu.make_async_copy(src, dst, load_sems.at[i])
        loads[name].start()
    barrier = pltpu.get_barrier_semaphore()
    partners = to_y[1:] + to_z[1:] + to_far + to_x[1:] + [to_core]
    for to in partners:
        pl.semaphore_signal(barrier, inc=1, device_id=to, device_id_type=MESH)
    pl.semaphore_wait(barrier, len(partners))

    loads["hidden"].wait()
    loads["ld"].wait()
    hid = hidden_ref[...].T
    rot = dot(hid, ld_ref[:, LATENT:])
    rot = jnp.concatenate([rot, jnp.zeros_like(rot)], axis=1)
    kv_y = []
    for d in (1, 3, 2):
        kv_out[d - 1, :, 0:128] = dot(hid, ld_ref[:, rows(ys[d] * 128, 128)]).astype(BF16)
        kv_out[d - 1, :, 128:256] = rot.astype(BF16)
        kv_y.append(wires.send(kv_out.at[d - 1], kv_in.at[d - 1], to_y[d]))
    l_cols = rows(y * 128, 128)
    q_cols = rows(y * 384, 384)
    kv_own[:, 0:128] = dot(hid, ld_ref[:, l_cols])
    kv_own[:, 128:256] = rot
    loads["qd"].wait()
    for d in (1, 3, 2):
        q_out[d - 1] = dot(hid, qd_ref[:, rows(ys[d] * 384, 384)]).astype(BF16)
    q_own[...] = dot(hid, qd_ref[:, q_cols])

    def over_y(copies, own, received):
        wait_all(copies)
        total = own[...]
        for d in range(NY - 1):
            total = total + received[d].astype(F32)
        own[...] = total
        return total

    def to_all_z(total, out, received):
        for i in range(NZ):
            out[i] = total[16 * i : 16 * i + 16].astype(BF16)
        return [wires.send(out.at[zs[d]], received.at[d - 1], to_z[d]) for d in FAR_FIRST]

    here = rows(z * 16, 16)

    def over_z(copies, own, received):
        wait_all(copies)
        total = own[here, :]
        for d in range(NZ - 1):
            total = total + received[d].astype(F32)
        return total

    kv_z = to_all_z(over_y(kv_y, kv_own, kv_in), kvz_out, kvz_in)
    q_y = [wires.send(q_out.at[d - 1], q_in.at[d - 1], to_y[d]) for d in (1, 3, 2)]
    loads["pos"].wait()
    loads["freq"].wait()
    freq = jnp.broadcast_to(freq_ref[...][None, :], (128, 128)).T[: ROPE // 2]
    angles = freq * pos_ref[...].astype(F32)[None, :]
    cosine, sine = jnp.cos(angles), jnp.sin(angles)
    cos_ref[...] = jnp.concatenate([cosine, cosine, cosine, cosine], axis=0).T
    sin_ref[...] = jnp.concatenate([-sine, sine, -sine, sine], axis=0).T
    loads["qg"].wait()
    loads["lg"].wait()
    gain_ref[...] = qg_ref[...][None, :]
    lgain_ref[...] = lg_ref[...][None, :]

    mine = over_z(kv_z, kv_own, kvz_in)
    lat, rot = mine[:, :128], mine[:, 128:]
    half = ROPE // 2
    swapped = jnp.concatenate([rot[:, half:ROPE], rot[:, :half]], axis=1)
    turned = rot[:, :ROPE] * cos_ref[here, :ROPE] + swapped * sin_ref[here, :ROPE]
    kz_ref[zh, here, 128:256] = jnp.concatenate([turned, jnp.zeros_like(turned)], axis=1).astype(BF16)
    kz_ref[zh, here, 0:128] = lat.astype(BF16)
    piece = kz_ref.at[zh, here]
    kz = [wires.send(piece, piece, to_z[d]) for d in FAR_FIRST]
    kz += [wires.send(piece, piece, to_far[d]) for d in range(NZ)]
    q_z = to_all_z(over_y(q_y, q_own, q_in), qz_out, qz_in)
    loads["wo"].wait()
    weights = []

    def share_weights(i):
        size = wo_ref.shape[1] // 4
        piece = wo_ref.at[y, i * size : i * size + size, :]
        weights.extend(wires.send(piece, piece, to_y[d]) for d in (1, 3, 2))

    share_weights(0)
    share_weights(1)

    def key_rows(d, i):
        return rows(ctx_of(lax.rem(x + NX - d, NX), i, core) * 128, 128)

    wait_all(kz)
    for i in range(2):
        k_ref[key_rows(0, i), l_cols] = kz_ref[i, :, 0:128]
        k_ref[key_rows(0, i), LATENT:KEY] = kz_ref[i, :, 128:256]

    def key_over_y(d, i):
        piece = k_ref.at[key_rows(d, i), l_cols]
        return [wires.send(piece, piece, to_y[e]) for e in (1, 3, 2)]

    first_y = key_over_y(0, 0)
    second_x, second_y = {}, {}
    for d in (1, 3, 2):
        second_x[d] = []
        for cols in (l_cols, pl.ds(LATENT, 128)):
            piece = k_ref.at[key_rows(0, 1), cols]
            second_x[d].append(wires.send(piece, piece, to_x[d]))
    second_y[0] = key_over_y(0, 1)
    q_low = over_z(q_z, q_own, qz_in)
    q_ref[here, q_cols] = (q_low * gain_ref[:, q_cols]).astype(BF16)
    piece = q_ref.at[here, q_cols]
    qz = [wires.send(piece, piece, to_z[d]) for d in FAR_FIRST]
    wait_all(first_y)
    first_x = {}
    for d in (1, 3, 2):
        piece = k_ref.at[key_rows(0, 0), :]
        first_x[d] = [wires.send(piece, piece, to_x[d])]
    wait_all(qz)
    piece = q_ref.at[:, q_cols]
    q_all = [wires.send(piece, piece, to_y[d]) for d in (1, 3, 2)]
    for d in (1, 3, 2):
        wait_all(second_x[d])
        second_y[d] = key_over_y(d, 1)

    key_core = {}

    def key_to_core(d):
        if d:
            wait_all(first_x[d])
        wait_all(second_y[d])
        key_core[d] = []
        for i in range(2):
            piece = k_ref.at[key_rows(d, i), :]
            key_core[d].append(wires.send(piece, piece, to_core))

    for name in ("qup", "ka", "va", "doc"):
        loads[name].wait()
    key_to_core(0)
    wait_all(q_all)
    plain = q_ref[...].astype(F32) / gain_ref[...]
    mean = jnp.sum(plain * plain, axis=1, keepdims=True) / QRANK
    full = dot(q_ref[...], qup_ref[...]) * lax.rsqrt(mean + 1e-06)
    lgain = lgain_ref[...]
    cosine, sine = cos_ref[:, :ROPE], sin_ref[:, :ROPE]
    for h in range(4):
        at = h * (NOPE + ROPE)
        nope = full[:, at : at + NOPE].astype(BF16)
        raw = full[:, at + NOPE : at + NOPE + ROPE]
        swapped = jnp.concatenate([raw[:, half:], raw[:, :half]], axis=1)
        turned = raw * cosine + swapped * sine
        low = dot_t(nope, ka_ref[:, h * NOPE : (h + 1) * NOPE])
        mine = slice(h * 128, h * 128 + 128)
        qc_ref[mine, :LATENT] = (low * lgain).astype(BF16)
        qc_ref[mine, LATENT:] = jnp.concatenate([turned, jnp.zeros_like(turned)], axis=1).astype(BF16)

    doc = jnp.broadcast_to(doc_ref[...].astype(F32)[None, :], (128, 128)).T[:, 0:1].astype(jnp.int32)
    query_index = ctx * 128 + lax.broadcasted_iota(jnp.int32, (128, 512), 0)
    key_lane = lax.broadcasted_iota(jnp.int32, (128, 512), 1)
    top = [None] * 4

    def scores(d):
        wait_all(key_core[d])
        at = rows(lax.rem(x + NX - d, NX) * 512, 512)
        key_index = key_lane + lax.rem(x + NX - d, NX) * 512
        bias = jnp.where((key_index <= query_index) & (key_index >= doc), 0.0, -1e30)
        keys = k_ref[at, :LATENT]
        wide = keys.astype(F32)
        mean = dot_t(jnp.ones((8, LATENT), BF16), (wide * wide).astype(BF16)) / LATENT
        factor = lax.rsqrt(mean + 1e-06)
        factor_ref[:, at] = factor
        factor = factor[0:1] * SCALE
        block = dot_t(qc_ref[:, :LATENT], keys)
        turn = dot_t(qc_ref[:, LATENT:], k_ref[at, LATENT:])
        for h in range(4):
            mine = slice(h * 128, h * 128 + 128)
            values = block[mine] * factor + (turn[mine] * SCALE + bias)
            s_ref[mine, at] = values
            most = jnp.max(values, axis=1, keepdims=True)
            top[h] = most if top[h] is None else jnp.maximum(top[h], most)

    key_to_core(1)
    scores(0)
    key_to_core(3)
    scores(1)
    key_to_core(2)
    scores(3)
    scores(2)

    cols = rows(y * 256, 256)

    def mix(pair):
        mine = slice(pair * 256, pair * 256 + 256)
        most = jnp.concatenate([top[2 * pair], top[2 * pair + 1]], axis=0)
        weighted = jnp.zeros((256, LATENT), F32)
        total = jnp.zeros((256, 1), F32)
        for j in range(4):
            span = slice(512 * j, 512 * j + 512)
            expo = jnp.exp(s_ref[mine, span] - most)
            total = total + jnp.sum(expo, axis=1, keepdims=True)
            expo = expo * factor_ref[0:1, span]
            weighted = weighted + dot(expo.astype(BF16), k_ref[span, :LATENT])
        mixed = (weighted * lgain / total).astype(BF16)
        for i in range(2):
            at = (2 * pair + i) * VDIM
            result = dot(mixed[128 * i : 128 * i + 128], va_ref[:, at : at + VDIM]).astype(BF16)
            for part in range(4):
                for side in range(2):
                    first = 64 * side + 16 * part
                    ho_ref[pair, part, side, :, 128 * i : 128 * i + 128] = result[first : first + 16]
        g_ref[pair, core, :, x, :, cols] = ho_ref[pair, y]
        spot = g_ref.at[pair, core, :, x, :, cols]
        return [wires.send(ho_ref.at[pair, ys[d]], spot, to_y[d]) for d in (1, 3, 2)]

    def block(pair, side, d):
        return g_ref.at[pair, core, side, lax.rem(x + NX - d, NX)]

    def far_block(pair, side, d):
        return g_ref.at[pair, 2 + core, side, lax.rem(x + NX - d, NX)]

    over_far, over_x, own_core, far_core = {}, {}, [], []

    def launch(pair, copies):
        wait_all(copies)
        for side in range(2):
            over_far[pair, side] = wires.send(
                block(pair, side, 0), far_block(pair, side, 0), to_far[0]
            )
        piece = block(pair, slice(None), 0)
        for d in (1, 3, 2):
            over_x[pair, d] = wires.send(piece, piece, to_x[d])
        own_core.append(wires.send(piece, piece, to_core))

    handed = [mix(0), mix(1)]
    launch(0, handed[0])
    launch(1, handed[1])
    share_weights(2)
    share_weights(3)

    def spread(pair):
        for side in range(2):
            over_far[pair, side].wait()
            piece = far_block(pair, side, 0)
            for d in (1, 3, 2):
                over_x[pair, side, d] = wires.send(piece, piece, to_x[d])
            far_core.append(wires.send(piece, piece, to_core))

    spread(0)
    for pair in range(2):
        for d in (1, 3, 2):
            over_x[pair, d].wait()
            piece = block(pair, slice(None), d)
            own_core.append(wires.send(piece, piece, to_core))
    spread(1)

    pair_at, odd = z // 2, z % 2
    near = (ctx, y * NZ + pair_at * 2 + 1 - odd)
    halves = {}
    last = wires.used + 8
    wires.used += 16

    def product(j):
        total = jnp.zeros((128, out_ref.shape[1]), F32)
        for pair in range(2):
            tokens = g_ref[pair, j].reshape(128, 1024)
            for i in range(NY):
                total = total + dot_t(
                    tokens[:, 256 * i : 256 * i + 256], wo_ref[i, :, 256 * pair : 256 * pair + 256]
                )
        for side in range(2):
            part = total[64 * side : 64 * side + 64]
            part = jnp.concatenate([part[:32], part[32:]], axis=1)
            own_ref[j, side] = part
            z_out[j, side] = part.astype(BF16)
        halves[j] = wires.send(z_out.at[j, 1 - odd], z_half.at[j], near)

    def pair_of(j):
        return 2 * (zh, other)[j // 2] + j % 2

    def pair_copy(j):
        away = lax.rem(pair_of(j) - pair_at + 4, 4)
        copy = pltpu.make_async_remote_copy(
            src_ref=pair_out.at[j],
            dst_ref=z_in.at[away],
            send_sem=send_sems.at[last + j],
            recv_sem=recv_sems.at[last + away],
            device_id=(ctx, y * NZ + pair_of(j) * 2 + odd),
            device_id_type=MESH,
        )
        return away, copy

    def pass_on(j):
        halves[j].wait()
        total = own_ref[j, odd] + z_half[j].astype(F32)
        own_ref[j, odd] = total
        pair_out[j] = total.astype(BF16)
        away, copy = pair_copy(j)

        @pl.when(away != 0)
        def _():
            copy.start()

    def forward(pair):
        for side in range(2):
            for d in (1, 3, 2):
                over_x[pair, side, d].wait()
                piece = far_block(pair, side, d)
                far_core.append(wires.send(piece, piece, to_core))

    wait_all(own_core)
    wait_all(weights)
    product(0)
    product(1)
    forward(0)
    pass_on(0)
    pass_on(1)
    forward(1)
    wait_all(far_core)
    product(2)
    product(3)
    pass_on(2)
    pass_on(3)
    half_at = pair_at // 2
    total = own_ref[pair_at % 2 + 2 * (half_at + zh - 2 * half_at * zh), odd]
    for away in (1, 3, 2):
        pltpu.make_async_remote_copy(
            src_ref=pair_out.at[0],
            dst_ref=z_in.at[away],
            send_sem=send_sems.at[last],
            recv_sem=recv_sems.at[last + away],
            device_id=near,
            device_id_type=MESH,
        ).wait_recv()
        total = total + z_in[away].astype(F32)
    for j in range(4):
        away, copy = pair_copy(j)

        @pl.when(away != 0)
        def _(copy=copy):
            copy.wait_send()
    width = out_ref.shape[1]
    result = jnp.concatenate([total[:, :width], total[:, width:]], axis=0).astype(BF16)
    for i in range(NX):
        fin_out[i] = result[16 * i : 16 * i + 16]
    fin_ref[y] = fin_out[y]
    wait_all([wires.send(fin_out.at[ys[d]], fin_ref.at[y], to_y[d]) for d in (1, 3, 2)])
    for i in range(NY):
        out_ref[16 * i : 16 * i + 16, :] = fin_ref[i]
    assert wires.used <= N_WIRES


def body(
    hidden,
    query_down,
    latent_down,
    query_gain,
    latent_gain,
    query_up,
    key_absorb,
    value_absorb,
    out_proj,
    doc_start,
    positions,
):
    half = ROPE // 2
    freqs = np.zeros((128,), np.float32)
    freqs[:half] = 10000.0 ** (-2.0 * np.arange(half) / ROPE)
    width = out_proj.shape[1]
    hidden, out_proj = hidden.T, out_proj.T
    vmem = pltpu.VMEM
    operands = (
        hidden,
        query_down,
        latent_down,
        query_gain,
        latent_gain,
        query_up,
        key_absorb,
        value_absorb,
        out_proj,
        doc_start,
        positions,
        jnp.asarray(freqs),
    )
    scratch = [vmem(a.shape, a.dtype) for a in operands]
    scratch[8] = vmem((NY,) + out_proj.shape, BF16)
    scratch += [
        vmem((1, QRANK), F32),
        vmem((1, LATENT), F32),
        vmem((128, 128), F32),
        vmem((128, 128), F32),
        vmem((3, 128, 256), BF16),
        vmem((3, 128, 256), BF16),
        vmem((3, 128, 384), BF16),
        vmem((3, 128, 384), BF16),
        vmem((128, 256), F32),
        vmem((128, 384), F32),
        vmem((8, 16, 256), BF16),
        vmem((7, 16, 256), BF16),
        vmem((8, 16, 384), BF16),
        vmem((7, 16, 384), BF16),
        vmem((2, 128, 256), BF16),
        vmem((128, QRANK), BF16),
        vmem((2048, KEY), BF16),
        vmem((512, KEY), BF16),
        vmem((512, 2048), F32),
        vmem((8, 2048), F32),
        vmem((2, 4, 2, 16, 256), BF16),
        vmem((2, 4, 2, 4, 16, 1024), BF16),
        vmem((4, 2, 32, 2 * width), F32),
        vmem((4, 2, 32, 2 * width), BF16),
        vmem((4, 32, 2 * width), BF16),
        vmem((4, 32, 2 * width), BF16),
        vmem((4, 32, 2 * width), BF16),
        vmem((4, 16, width), BF16),
        vmem((4, 16, width), BF16),
        pltpu.SemaphoreType.DMA((len(operands),)),
        pltpu.SemaphoreType.DMA((N_WIRES,)),
        pltpu.SemaphoreType.DMA((N_WIRES,)),
    ]
    return pl.pallas_call(
        kernel,
        out_shape=jax.ShapeDtypeStruct((64, width), BF16),
        in_specs=[pl.BlockSpec(memory_space=pl.ANY)] * len(operands),
        out_specs=pl.BlockSpec(memory_space=pltpu.VMEM),
        scratch_shapes=scratch,
        compiler_params=pltpu.CompilerParams(
            collective_id=0, has_side_effects=True, vmem_limit_bytes=VMEM_BYTES
        ),
        name="latent_attention",
    )(*operands)


def solution(mesh):
    in_specs = (
        P("ctx", "head"),
        P("head", None),
        P("head", None),
        P(),
        P(),
        P(None, "head"),
        P(None, "head"),
        P(None, "head"),
        P("head", "ctx"),
        P("ctx"),
        P("ctx"),
    )
    out_specs = P("head", "ctx")
    return jax.shard_map(body, mesh=mesh, in_specs=in_specs, out_specs=out_specs, check_vma=False)
```

```python
import jax
import jax.numpy as jnp
import numpy as np
from jax import lax
from jax.experimental import pallas as pl
from jax.experimental.pallas import tpu as pltpu
from jax.sharding import PartitionSpec as P

LATENT = 512
ROPE = 64
NOPE = 128
VDIM = 128
QRANK = 1536
NX, NY, NZ = 4, 4, 8
KEY = LATENT + 2 * ROPE
SCALE = (NOPE + ROPE) ** (-0.5)
MESH = pl.DeviceIdType.MESH
BF16 = jnp.bfloat16
F32 = jnp.float32
FAR_FIRST = (4, 5, 3, 6, 2, 7, 1)
N_WIRES = 224
VMEM_BYTES = 60 * 1024 * 1024


def dot(a, b):
    return jnp.dot(a, b, preferred_element_type=F32)


def dot_t(a, b):
    return lax.dot_general(a, b, (((1,), (1,)), ((), ())), preferred_element_type=F32)


def rows(start, size):
    return pl.ds(pl.multiple_of(start, size), size)


def ctx_of(x, zh, core):
    return x * 4 + zh * 2 + core


class Wires:
    def __init__(self, send_sems, recv_sems):
        self.send_sems, self.recv_sems, self.used = send_sems, recv_sems, 0

    def send(self, src, dst, to):
        at = self.used
        self.used += 1
        copy = pltpu.make_async_remote_copy(
            src_ref=src,
            dst_ref=dst,
            send_sem=self.send_sems.at[at],
            recv_sem=self.recv_sems.at[at],
            device_id=to,
            device_id_type=MESH,
        )
        copy.start()
        return copy


def wait_all(copies):
    for copy in copies:
        copy.wait()


def kernel(
    hidden_hbm,
    qd_hbm,
    ld_hbm,
    qg_hbm,
    lg_hbm,
    qup_hbm,
    ka_hbm,
    va_hbm,
    wo_hbm,
    doc_hbm,
    pos_hbm,
    freq_hbm,
    out_ref,
    hidden_ref,
    qd_ref,
    ld_ref,
    qg_ref,
    lg_ref,
    qup_ref,
    ka_ref,
    va_ref,
    wo_ref,
    doc_ref,
    pos_ref,
    freq_ref,
    gain_ref,
    lgain_ref,
    cos_ref,
    sin_ref,
    kv_out,
    kv_in,
    q_out,
    q_in,
    kv_own,
    q_own,
    kvz_out,
    kvz_in,
    qz_out,
    qz_in,
    kz_ref,
    q_ref,
    k_ref,
    qc_ref,
    s_ref,
    factor_ref,
    ho_ref,
    g_ref,
    own_ref,
    z_out,
    z_half,
    pair_out,
    z_in,
    fin_out,
    fin_ref,
    load_sems,
    send_sems,
    recv_sems,
):
    ctx = lax.axis_index("ctx")
    head = lax.axis_index("head")
    x, zh, core = ctx // 4, (ctx // 2) % 2, ctx % 2
    y, z = head // NZ, head % NZ
    ys = [lax.rem(y + d, NY) for d in range(NY)]
    zs = [lax.rem(z + d, NZ) for d in range(NZ)]
    other = 1 - zh
    far = ctx_of(x, other, core)
    to_y = [(ctx, ys[d] * NZ + z) for d in range(NY)]
    to_z = [(ctx, y * NZ + zs[d]) for d in range(NZ)]
    to_far = [(far, y * NZ + zs[d]) for d in range(NZ)]
    to_x = [(ctx_of(lax.rem(x + d, NX), zh, core), head) for d in range(NX)]
    to_core = (ctx_of(x, zh, 1 - core), head)
    wires = Wires(send_sems, recv_sems)

    loads = {}
    for i, (name, src, dst) in enumerate(
        [
            ("hidden", hidden_hbm, hidden_ref),
            ("ld", ld_hbm, ld_ref),
            ("qd", qd_hbm, qd_ref),
            ("qg", qg_hbm, qg_ref),
            ("lg", lg_hbm, lg_ref),
            ("pos", pos_hbm, pos_ref),
            ("doc", doc_hbm, doc_ref),
            ("freq", freq_hbm, freq_ref),
            ("qup", qup_hbm, qup_ref),
            ("ka", ka_hbm, ka_ref),
            ("va", va_hbm, va_ref),
            ("wo", wo_hbm, wo_ref.at[y]),
        ]
    ):
        loads[name] = pltpu.make_async_copy(src, dst, load_sems.at[i])
        loads[name].start()
    barrier = pltpu.get_barrier_semaphore()
    partners = to_y[1:] + to_z[1:] + to_far + to_x[1:] + [to_core]
    for to in partners:
        pl.semaphore_signal(barrier, inc=1, device_id=to, device_id_type=MESH)
    pl.semaphore_wait(barrier, len(partners))

    loads["hidden"].wait()
    loads["ld"].wait()
    hid = hidden_ref[...].T
    rot = dot(hid, ld_ref[:, LATENT:])
    rot = jnp.concatenate([rot, jnp.zeros_like(rot)], axis=1)
    kv_y = []
    for d in (1, 3, 2):
        kv_out[d - 1, :, 0:128] = dot(hid, ld_ref[:, rows(ys[d] * 128, 128)]).astype(BF16)
        kv_out[d - 1, :, 128:256] = rot.astype(BF16)
        kv_y.append(wires.send(kv_out.at[d - 1], kv_in.at[d - 1], to_y[d]))
    l_cols = rows(y * 128, 128)
    q_cols = rows(y * 384, 384)
    kv_own[:, 0:128] = dot(hid, ld_ref[:, l_cols])
    kv_own[:, 128:256] = rot
    loads["qd"].wait()
    for d in (1, 3, 2):
        q_out[d - 1] = dot(hid, qd_ref[:, rows(ys[d] * 384, 384)]).astype(BF16)
    q_own[...] = dot(hid, qd_ref[:, q_cols])

    def over_y(copies, own, received):
        wait_all(copies)
        total = own[...]
        for d in range(NY - 1):
            total = total + received[d].astype(F32)
        own[...] = total
        return total

    def to_all_z(total, out, received):
        for i in range(NZ):
            out[i] = total[16 * i : 16 * i + 16].astype(BF16)
        return [wires.send(out.at[zs[d]], received.at[d - 1], to_z[d]) for d in FAR_FIRST]

    here = rows(z * 16, 16)

    def over_z(copies, own, received):
        wait_all(copies)
        total = own[here, :]
        for d in range(NZ - 1):
            total = total + received[d].astype(F32)
        return total

    kv_z = to_all_z(over_y(kv_y, kv_own, kv_in), kvz_out, kvz_in)
    q_y = [wires.send(q_out.at[d - 1], q_in.at[d - 1], to_y[d]) for d in (1, 3, 2)]
    loads["pos"].wait()
    loads["freq"].wait()
    freq = jnp.broadcast_to(freq_ref[...][None, :], (128, 128)).T[: ROPE // 2]
    angles = freq * pos_ref[...].astype(F32)[None, :]
    cosine, sine = jnp.cos(angles), jnp.sin(angles)
    cos_ref[...] = jnp.concatenate([cosine, cosine, cosine, cosine], axis=0).T
    sin_ref[...] = jnp.concatenate([-sine, sine, -sine, sine], axis=0).T
    loads["qg"].wait()
    loads["lg"].wait()
    gain_ref[...] = qg_ref[...][None, :]
    lgain_ref[...] = lg_ref[...][None, :]

    mine = over_z(kv_z, kv_own, kvz_in)
    lat, rot = mine[:, :128], mine[:, 128:]
    half = ROPE // 2
    swapped = jnp.concatenate([rot[:, half:ROPE], rot[:, :half]], axis=1)
    turned = rot[:, :ROPE] * cos_ref[here, :ROPE] + swapped * sin_ref[here, :ROPE]
    kz_ref[zh, here, 128:256] = jnp.concatenate([turned, jnp.zeros_like(turned)], axis=1).astype(BF16)
    kz_ref[zh, here, 0:128] = lat.astype(BF16)
    piece = kz_ref.at[zh, here]
    kz = [wires.send(piece, piece, to_z[d]) for d in FAR_FIRST]
    kz += [wires.send(piece, piece, to_far[d]) for d in range(NZ)]
    q_z = to_all_z(over_y(q_y, q_own, q_in), qz_out, qz_in)
    loads["wo"].wait()
    weights = []

    def share_weights(i):
        size = wo_ref.shape[1] // 4
        piece = wo_ref.at[y, i * size : i * size + size, :]
        weights.extend(wires.send(piece, piece, to_y[d]) for d in (1, 3, 2))

    share_weights(0)
    share_weights(1)

    def key_rows(d, i):
        return rows(ctx_of(lax.rem(x + NX - d, NX), i, core) * 128, 128)

    wait_all(kz)
    for i in range(2):
        k_ref[key_rows(0, i), l_cols] = kz_ref[i, :, 0:128]
        k_ref[key_rows(0, i), LATENT:KEY] = kz_ref[i, :, 128:256]

    def key_over_y(d, i):
        piece = k_ref.at[key_rows(d, i), l_cols]
        return [wires.send(piece, piece, to_y[e]) for e in (1, 3, 2)]

    first_y = key_over_y(0, 0)
    second_x, second_y = {}, {}
    for d in (1, 3, 2):
        second_x[d] = []
        for cols in (l_cols, pl.ds(LATENT, 128)):
            piece = k_ref.at[key_rows(0, 1), cols]
            second_x[d].append(wires.send(piece, piece, to_x[d]))
    second_y[0] = key_over_y(0, 1)
    q_low = over_z(q_z, q_own, qz_in)
    q_ref[here, q_cols] = (q_low * gain_ref[:, q_cols]).astype(BF16)
    piece = q_ref.at[here, q_cols]
    qz = [wires.send(piece, piece, to_z[d]) for d in FAR_FIRST]
    wait_all(first_y)
    first_x = {}
    for d in (1, 3, 2):
        piece = k_ref.at[key_rows(0, 0), :]
        first_x[d] = [wires.send(piece, piece, to_x[d])]
    wait_all(qz)
    piece = q_ref.at[:, q_cols]
    q_all = [wires.send(piece, piece, to_y[d]) for d in (1, 3, 2)]
    for d in (1, 3, 2):
        wait_all(second_x[d])
        second_y[d] = key_over_y(d, 1)

    key_core = {}

    def key_to_core(d):
        if d:
            wait_all(first_x[d])
        wait_all(second_y[d])
        key_core[d] = []
        for i in range(2):
            piece = k_ref.at[key_rows(d, i), :]
            key_core[d].append(wires.send(piece, piece, to_core))

    for name in ("qup", "ka", "va", "doc"):
        loads[name].wait()
    for d in (0, 1, 3, 2):
        key_to_core(d)
    wait_all(q_all)
    plain = q_ref[...].astype(F32) / gain_ref[...]
    mean = jnp.sum(plain * plain, axis=1, keepdims=True) / QRANK
    full = dot(q_ref[...], qup_ref[...]) * lax.rsqrt(mean + 1e-06)
    lgain = lgain_ref[...]
    cosine, sine = cos_ref[:, :ROPE], sin_ref[:, :ROPE]
    for h in range(4):
        at = h * (NOPE + ROPE)
        nope = full[:, at : at + NOPE].astype(BF16)
        raw = full[:, at + NOPE : at + NOPE + ROPE]
        swapped = jnp.concatenate([raw[:, half:], raw[:, :half]], axis=1)
        turned = raw * cosine + swapped * sine
        low = dot_t(nope, ka_ref[:, h * NOPE : (h + 1) * NOPE])
        mine = slice(h * 128, h * 128 + 128)
        qc_ref[mine, :LATENT] = (low * lgain).astype(BF16)
        qc_ref[mine, LATENT:] = jnp.concatenate([turned, jnp.zeros_like(turned)], axis=1).astype(BF16)

    doc = jnp.broadcast_to(doc_ref[...].astype(F32)[None, :], (128, 128)).T[:, 0:1].astype(jnp.int32)
    query_index = ctx * 128 + lax.broadcasted_iota(jnp.int32, (128, 512), 0)
    key_lane = lax.broadcasted_iota(jnp.int32, (128, 512), 1)
    top = [None] * 4

    def scores(d):
        wait_all(key_core[d])
        at = rows(lax.rem(x + NX - d, NX) * 512, 512)
        key_index = key_lane + lax.rem(x + NX - d, NX) * 512
        bias = jnp.where((key_index <= query_index) & (key_index >= doc), 0.0, -1e30)
        keys = k_ref[at, :LATENT]
        wide = keys.astype(F32)
        mean = dot_t(jnp.ones((8, LATENT), BF16), (wide * wide).astype(BF16)) / LATENT
        factor = lax.rsqrt(mean + 1e-06)
        factor_ref[:, at] = factor
        factor = factor[0:1] * SCALE
        block = dot_t(qc_ref[:, :LATENT], keys)
        turn = dot_t(qc_ref[:, LATENT:], k_ref[at, LATENT:])
        for h in range(4):
            mine = slice(h * 128, h * 128 + 128)
            values = block[mine] * factor + (turn[mine] * SCALE + bias)
            s_ref[mine, at] = values
            most = jnp.max(values, axis=1, keepdims=True)
            top[h] = most if top[h] is None else jnp.maximum(top[h], most)

    scores(0)
    scores(1)
    scores(3)
    scores(2)

    cols = rows(y * 256, 256)

    def mix(pair):
        mine = slice(pair * 256, pair * 256 + 256)
        most = jnp.concatenate([top[2 * pair], top[2 * pair + 1]], axis=0)
        weighted = jnp.zeros((256, LATENT), F32)
        total = jnp.zeros((256, 1), F32)
        for j in range(4):
            span = slice(512 * j, 512 * j + 512)
            expo = jnp.exp(s_ref[mine, span] - most)
            total = total + jnp.sum(expo, axis=1, keepdims=True)
            expo = expo * factor_ref[0:1, span]
            weighted = weighted + dot(expo.astype(BF16), k_ref[span, :LATENT])
        mixed = (weighted * lgain / total).astype(BF16)
        for i in range(2):
            at = (2 * pair + i) * VDIM
            result = dot(mixed[128 * i : 128 * i + 128], va_ref[:, at : at + VDIM]).astype(BF16)
            for part in range(4):
                for side in range(2):
                    first = 64 * side + 16 * part
                    ho_ref[pair, part, side, :, 128 * i : 128 * i + 128] = result[first : first + 16]
        g_ref[pair, core, :, x, :, cols] = ho_ref[pair, y]
        spot = g_ref.at[pair, core, :, x, :, cols]
        return [wires.send(ho_ref.at[pair, ys[d]], spot, to_y[d]) for d in (1, 3, 2)]

    def block(pair, side, d):
        return g_ref.at[pair, core, side, lax.rem(x + NX - d, NX)]

    def far_block(pair, side, d):
        return g_ref.at[pair, 2 + core, side, lax.rem(x + NX - d, NX)]

    over_far, over_x, own_core, far_core = {}, {}, [], []

    def launch(pair, copies):
        wait_all(copies)
        for side in range(2):
            over_far[pair, side] = wires.send(
                block(pair, side, 0), far_block(pair, side, 0), to_far[0]
            )
        piece = block(pair, slice(None), 0)
        for d in (1, 3, 2):
            over_x[pair, d] = wires.send(piece, piece, to_x[d])
        own_core.append(wires.send(piece, piece, to_core))

    handed = [mix(0), mix(1)]
    launch(0, handed[0])
    launch(1, handed[1])
    share_weights(2)
    share_weights(3)

    def spread(pair):
        for side in range(2):
            over_far[pair, side].wait()
            piece = far_block(pair, side, 0)
            for d in (1, 3, 2):
                over_x[pair, side, d] = wires.send(piece, piece, to_x[d])
            far_core.append(wires.send(piece, piece, to_core))

    spread(0)
    for pair in range(2):
        for d in (1, 3, 2):
            over_x[pair, d].wait()
            piece = block(pair, slice(None), d)
            own_core.append(wires.send(piece, piece, to_core))
    spread(1)

    pair_at, odd = z // 2, z % 2
    near = (ctx, y * NZ + pair_at * 2 + 1 - odd)
    halves = {}
    last = wires.used + 8
    wires.used += 16

    def product(j):
        total = jnp.zeros((128, out_ref.shape[1]), F32)
        for pair in range(2):
            tokens = g_ref[pair, j].reshape(128, 1024)
            for i in range(NY):
                total = total + dot_t(
                    tokens[:, 256 * i : 256 * i + 256], wo_ref[i, :, 256 * pair : 256 * pair + 256]
                )
        for side in range(2):
            part = total[64 * side : 64 * side + 64]
            part = jnp.concatenate([part[:32], part[32:]], axis=1)
            own_ref[j, side] = part
            z_out[j, side] = part.astype(BF16)
        halves[j] = wires.send(z_out.at[j, 1 - odd], z_half.at[j], near)

    def pair_of(j):
        return 2 * (zh, other)[j // 2] + j % 2

    def pair_copy(j):
        away = lax.rem(pair_of(j) - pair_at + 4, 4)
        copy = pltpu.make_async_remote_copy(
            src_ref=pair_out.at[j],
            dst_ref=z_in.at[away],
            send_sem=send_sems.at[last + j],
            recv_sem=recv_sems.at[last + away],
            device_id=(ctx, y * NZ + pair_of(j) * 2 + odd),
            device_id_type=MESH,
        )
        return away, copy

    def pass_on(j):
        halves[j].wait()
        total = own_ref[j, odd] + z_half[j].astype(F32)
        own_ref[j, odd] = total
        pair_out[j] = total.astype(BF16)
        away, copy = pair_copy(j)

        @pl.when(away != 0)
        def _():
            copy.start()

    def forward(pair):
        for side in range(2):
            for d in (1, 3, 2):
                over_x[pair, side, d].wait()
                piece = far_block(pair, side, d)
                far_core.append(wires.send(piece, piece, to_core))

    wait_all(own_core)
    wait_all(weights)
    product(0)
    product(1)
    forward(0)
    pass_on(0)
    pass_on(1)
    forward(1)
    wait_all(far_core)
    product(2)
    product(3)
    pass_on(2)
    pass_on(3)
    half_at = pair_at // 2
    total = own_ref[pair_at % 2 + 2 * (half_at + zh - 2 * half_at * zh), odd]
    for away in (1, 3, 2):
        pltpu.make_async_remote_copy(
            src_ref=pair_out.at[0],
            dst_ref=z_in.at[away],
            send_sem=send_sems.at[last],
            recv_sem=recv_sems.at[last + away],
            device_id=near,
            device_id_type=MESH,
        ).wait_recv()
        total = total + z_in[away].astype(F32)
    for j in range(4):
        away, copy = pair_copy(j)

        @pl.when(away != 0)
        def _(copy=copy):
            copy.wait_send()
    width = out_ref.shape[1]
    result = jnp.concatenate([total[:, :width], total[:, width:]], axis=0).astype(BF16)
    for i in range(NX):
        fin_out[i] = result[16 * i : 16 * i + 16]
    fin_ref[y] = fin_out[y]
    wait_all([wires.send(fin_out.at[ys[d]], fin_ref.at[y], to_y[d]) for d in (1, 3, 2)])
    for i in range(NY):
        out_ref[16 * i : 16 * i + 16, :] = fin_ref[i]
    assert wires.used <= N_WIRES


def body(
    hidden,
    query_down,
    latent_down,
    query_gain,
    latent_gain,
    query_up,
    key_absorb,
    value_absorb,
    out_proj,
    doc_start,
    positions,
):
    half = ROPE // 2
    freqs = np.zeros((128,), np.float32)
    freqs[:half] = 10000.0 ** (-2.0 * np.arange(half) / ROPE)
    width = out_proj.shape[1]
    hidden, out_proj = hidden.T, out_proj.T
    vmem = pltpu.VMEM
    operands = (
        hidden,
        query_down,
        latent_down,
        query_gain,
        latent_gain,
        query_up,
        key_absorb,
        value_absorb,
        out_proj,
        doc_start,
        positions,
        jnp.asarray(freqs),
    )
    scratch = [vmem(a.shape, a.dtype) for a in operands]
    scratch[8] = vmem((NY,) + out_proj.shape, BF16)
    scratch += [
        vmem((1, QRANK), F32),
        vmem((1, LATENT), F32),
        vmem((128, 128), F32),
        vmem((128, 128), F32),
        vmem((3, 128, 256), BF16),
        vmem((3, 128, 256), BF16),
        vmem((3, 128, 384), BF16),
        vmem((3, 128, 384), BF16),
        vmem((128, 256), F32),
        vmem((128, 384), F32),
        vmem((8, 16, 256), BF16),
        vmem((7, 16, 256), BF16),
        vmem((8, 16, 384), BF16),
        vmem((7, 16, 384), BF16),
        vmem((2, 128, 256), BF16),
        vmem((128, QRANK), BF16),
        vmem((2048, KEY), BF16),
        vmem((512, KEY), BF16),
        vmem((512, 2048), F32),
        vmem((8, 2048), F32),
        vmem((2, 4, 2, 16, 256), BF16),
        vmem((2, 4, 2, 4, 16, 1024), BF16),
        vmem((4, 2, 32, 2 * width), F32),
        vmem((4, 2, 32, 2 * width), BF16),
        vmem((4, 32, 2 * width), BF16),
        vmem((4, 32, 2 * width), BF16),
        vmem((4, 32, 2 * width), BF16),
        vmem((4, 16, width), BF16),
        vmem((4, 16, width), BF16),
        pltpu.SemaphoreType.DMA((len(operands),)),
        pltpu.SemaphoreType.DMA((N_WIRES,)),
        pltpu.SemaphoreType.DMA((N_WIRES,)),
    ]
    return pl.pallas_call(
        kernel,
        out_shape=jax.ShapeDtypeStruct((64, width), BF16),
        in_specs=[pl.BlockSpec(memory_space=pl.ANY)] * len(operands),
        out_specs=pl.BlockSpec(memory_space=pltpu.VMEM),
        scratch_shapes=scratch,
        compiler_params=pltpu.CompilerParams(
            collective_id=0, has_side_effects=True, vmem_limit_bytes=VMEM_BYTES
        ),
        name="latent_attention",
    )(*operands)


def solution(mesh):
    in_specs = (
        P("ctx", "head"),
        P("head", None),
        P("head", None),
        P(),
        P(),
        P(None, "head"),
        P(None, "head"),
        P(None, "head"),
        P("head", "ctx"),
        P("ctx"),
        P("ctx"),
    )
    out_specs = P("head", "ctx")
    return jax.shard_map(body, mesh=mesh, in_specs=in_specs, out_specs=out_specs, check_vma=False)
```
